256 devices in a mesh: dp: 2 (over core), row: 16 (over z_lo, x), col: 8 (over y, z_hi).
Axes of the slice: x: 4, y: 4, z: 8 (z_hi: 2, z_lo: 4; z = z_hi * 4 + z_lo), core: 2. Of those that a mesh axis runs over, the one named last changes fastest.
Arguments:
- tokens: bfloat16 [1024, 8192], P('dp', 'row'), may hold values from -6 to 6
- quantized_levels: int32 [2, 4096, 28672], P(None, 'row', 'col'), may hold values from 0 to 255
- block_scale_table: float32 [2, 128, 28672], P(None, 'row', 'col'), may hold values from 0.004 to 0.06
- adapter_down: bfloat16 [8192, 128], P('row'), may hold values from -0.0625 to 0.0625
- adapter_up: bfloat16 [2, 64, 28672], P(None, None, 'col'), may hold values from -0.75 to 0.75
- magnitude: float32 [2, 28672], P(None, 'col'), may hold values from 0.5 to 2
- output_gradient: bfloat16 [1024, 28672], P('dp', 'col'), may hold values from -6 to 6
Outputs:
- token_gradient: bfloat16 [1024, 8192], P(('dp', 'col'), 'row')
- adapter_down_gradient: float32 [8192, 128], P('row')
- adapter_up_gradient: float32 [2, 64, 28672], P(None, None, 'col')
- magnitude_gradient: float32 [2, 28672], P(None, 'col')
The draws below stay inside these ranges and needn't reach their ends.
All inputs are finite; a program needn't handle non-finite values.
Results may differ from the reference program's by a relative error of at most 0.0066.
Values may be sent and summed in bfloat16 or wider, within the bound.
A program may use at most 128 MiB of HBM per device.

```python
import math
import jax
import jax.numpy as jnp
from jax import lax

MODEL_WIDTH = 8192
HIDDEN_UNITS = 28672
ADAPTER_RANK = 64
TOKENS = 1024


def place_ends(array, key, smallest, largest):
    longest = array.shape.index(max(array.shape))
    spots = []
    for shift in (0, 1):
        where = [jax.random.randint(jax.random.fold_in(key, axis), (), 0, length) for axis, length in enumerate(array.shape)]
        where[longest] = (where[longest] + shift) % array.shape[longest]
        spots.append(tuple(where))
    return array.at[spots[0]].set(smallest).at[spots[1]].set(largest)


def spiked(array, rng, source, target, shards_of, factor):
    owner, partner = [(jnp.arange(array.shape[axis_at]) // (array.shape[axis_at] // shards_of)).reshape([-1 if axis == axis_at else 1 for axis in range(array.ndim)]) for axis_at in (source, target)]
    chosen = jax.random.permutation(rng, shards_of)[partner]
    strong = (owner == chosen) | (owner == (partner + shards_of // 2) % shards_of)
    return jnp.where(strong, factor * array, array)


def block_scale(rng, dims, cuts, low, top_value):
    def one(axis_at, blocks):
        heights = jax.random.uniform(jax.random.fold_in(jax.random.fold_in(rng, 6), axis_at), (blocks,), jnp.float32, low / len(cuts), top_value / len(cuts))
        return jnp.repeat(jnp.exp(heights), dims[axis_at] // blocks).reshape((-1,) + (1,) * (len(dims) - axis_at - 1))

    loudness = one(*cuts[0])
    for cut in cuts[1:]:
        loudness = loudness * one(*cut)
    return loudness


def noise(key, dims, deviation, bound, shards=(), kind=jnp.bfloat16):
    entries = jax.random.normal(key, dims, jnp.float32) * deviation
    if len(shards) > 0:
        entries = block_scale(key, dims, shards, -0.22, 0.18) * entries
    return jnp.clip(entries, min=-bound, max=bound).astype(kind)


def noise_with(own_key, extent, width, reach, cuts, heavy, held_as=jnp.bfloat16):
    entries = width * jax.random.normal(own_key, extent, jnp.float32)
    if cuts:
        entries = entries * block_scale(own_key, extent, cuts, -0.22, 0.18)
    return jnp.clip(spiked(entries, jax.random.fold_in(own_key, 3), *heavy), -reach, reach).astype(held_as)


def setup_inputs(seed: int = 0) -> dict:
    arg_keys = jax.random.split(jax.random.key(seed), 8)
    tokens = noise(arg_keys[0], (TOKENS, MODEL_WIDTH), 1.0, 6.0, ((0, 2), (1, 16)))
    quantized_levels = place_ends(jax.random.randint(arg_keys[1], (2, MODEL_WIDTH // 2, HIDDEN_UNITS), 0, 256), jax.random.fold_in(arg_keys[1], 1), 0, 255).astype(jnp.int32)
    block_scale_table = jnp.clip(jnp.exp(math.log(0.06) - 2.70805 * jax.random.uniform(arg_keys[2], (2, MODEL_WIDTH // 64, HIDDEN_UNITS), jnp.float32) ** block_scale(arg_keys[2], (2, MODEL_WIDTH // 64, HIDDEN_UNITS), ((1, 16), (2, 8)), -0.2, 0.2)), 0.004, 0.06)
    adapter_down = noise(arg_keys[3], (MODEL_WIDTH, 2 * ADAPTER_RANK), MODEL_WIDTH ** -0.5, 0.0625, ((0, 16),))
    adapter_up = noise(arg_keys[4], (2, ADAPTER_RANK, HIDDEN_UNITS), ADAPTER_RANK ** -0.5, 0.75, ((2, 8),))
    magnitude = jnp.clip(jnp.exp(math.log(2.0) - 1.3862944 * jax.random.uniform(arg_keys[5], (2, HIDDEN_UNITS), jnp.float32) ** block_scale(arg_keys[5], (2, HIDDEN_UNITS), ((1, 8),), -0.2, 0.2)), 0.5, 2.0)
    output_gradient = noise_with(arg_keys[6], (TOKENS, HIDDEN_UNITS), 1.0, 6.0, ((0, 2), (1, 8)), (1, 0, 8, 2.0))
    return {"tokens": tokens, "quantized_levels": quantized_levels, "block_scale_table": block_scale_table, "adapter_down": adapter_down, "adapter_up": adapter_up, "magnitude": magnitude, "output_gradient": output_gradient}


normal_levels = (-1.0, -0.6961928009986877, -0.5250730514526367, -0.39491748809814453, -0.28444138169288635, -0.18477343022823334, -0.09105003625154495, 0.0, 0.07958029955625534, 0.16093020141124725, 0.24611230194568634, 0.33791524171829224, 0.44070982933044434, 0.5626170039176941, 0.7229568362236023, 1.0)
adapter_scale = 2.0
norm_eps = 1e-06

def decode(quantized_levels, block_scale_table):
    pieces = [jnp.bitwise_and(jnp.right_shift(quantized_levels, 4 * k), 15) for k in range(2)]
    nibble = jnp.stack(pieces, axis=2).reshape(quantized_levels.shape[0], quantized_levels.shape[1] * 2, quantized_levels.shape[2])
    levels = jnp.zeros(nibble.shape, block_scale_table.dtype)
    for k in range(16):
        levels = jnp.where(nibble == k, normal_levels[k], levels)
    blocks = levels.reshape(quantized_levels.shape[0], block_scale_table.shape[1], -1, quantized_levels.shape[2]) * block_scale_table[:, :, None, :]
    return blocks.reshape(nibble.shape)

def branch_grads_of(pre_scale, output_gradient, factor):
    gate_value = pre_scale[:, 0] * factor[0]
    up_value = pre_scale[:, 1] * factor[1]
    sigmoid_gate = jax.nn.sigmoid(gate_value)
    grad_f = output_gradient.astype(jnp.float32)
    grad_gate = grad_f * up_value * sigmoid_gate * (1.0 + gate_value * (1.0 - sigmoid_gate))
    grad_up = grad_f * gate_value * sigmoid_gate
    return jnp.stack([grad_gate, grad_up], axis=1)

def reference(tokens, quantized_levels, block_scale_table, adapter_down, adapter_up, magnitude, output_gradient):
    block_span_width = math.gcd(HIDDEN_UNITS, 1024)
    block_count = HIDDEN_UNITS // block_span_width
    inner_rank_rows = jnp.dot(tokens, adapter_down, preferred_element_type=jnp.float32).astype(jnp.bfloat16)
    inner_float_rows = inner_rank_rows.astype(jnp.float32).reshape(-1, 2, ADAPTER_RANK)
    token_float_rows = tokens.astype(jnp.float32)

    def block(totals, block_index):
        token_input_gradient, backward_rank_rows = totals
        column_offset = block_index * block_span_width
        code_blk = lax.dynamic_slice_in_dim(quantized_levels, column_offset, block_span_width, 2)
        scale_blk = lax.dynamic_slice_in_dim(block_scale_table, column_offset, block_span_width, 2)
        adapter_up_block = lax.dynamic_slice_in_dim(adapter_up, column_offset, block_span_width, 2)
        mag_blk = lax.dynamic_slice_in_dim(magnitude, column_offset, block_span_width, 1)
        grad_blk = lax.dynamic_slice_in_dim(output_gradient, column_offset, block_span_width, 1)
        dequant_weight = decode(code_blk, scale_blk)
        combined_weight = jnp.stack([(dequant_weight[branch_index] + adapter_scale * jnp.dot(adapter_down[:, branch_index * ADAPTER_RANK:(branch_index + 1) * ADAPTER_RANK], adapter_up_block[branch_index], preferred_element_type=jnp.float32)).astype(jnp.bfloat16) for branch_index in range(2)])
        merged_f = combined_weight.astype(jnp.float32)
        col_norm = jnp.sqrt(lax.optimization_barrier(jnp.sum(merged_f * merged_f, axis=1)) + norm_eps)
        factor = mag_blk / col_norm
        pre_scale = jnp.einsum('td,pdf->tpf', token_float_rows, merged_f)
        branch_grads = branch_grads_of(pre_scale, grad_blk, factor)
        rescaled_weight = (branch_grads * factor[None]).astype(jnp.bfloat16)
        rescaled_float = rescaled_weight.astype(jnp.float32)
        grad_mag = lax.optimization_barrier(jnp.sum(branch_grads * pre_scale, axis=0)) / col_norm
        gradient_up_factor = adapter_scale * jnp.einsum('ynk,yna->nka', inner_float_rows, rescaled_float)
        backward_rank_rows = backward_rank_rows + jnp.einsum('yix,iex->yie', rescaled_float, adapter_up_block.astype(jnp.float32))
        token_input_gradient = token_input_gradient + jnp.einsum('tpf,pdf->td', rescaled_float, merged_f)
        return ((token_input_gradient, backward_rank_rows), (grad_mag, gradient_up_factor))
    init = (jnp.zeros((TOKENS, MODEL_WIDTH), jnp.float32), jnp.zeros((TOKENS, 2, ADAPTER_RANK), jnp.float32))
    (token_input_gradient, backward_rank_rows), (mags, up_factor_gradients) = lax.scan(block, init, jnp.arange(block_count, dtype=jnp.int32))
    magnitude_gradient = jnp.moveaxis(mags, 0, 1).reshape(2, HIDDEN_UNITS)
    adapter_up_gradient = jnp.moveaxis(up_factor_gradients, 0, 2).reshape(2, ADAPTER_RANK, HIDDEN_UNITS)
    backward_rank_rows = backward_rank_rows.reshape(TOKENS, 2 * ADAPTER_RANK).astype(jnp.bfloat16)
    adapter_down_gradient = adapter_scale * jnp.einsum('iz,iy->zy', token_float_rows, backward_rank_rows.astype(jnp.float32))
    return (token_input_gradient.astype(jnp.bfloat16), adapter_down_gradient, adapter_up_gradient, magnitude_gradient)
```

```python
import functools

import jax
import jax.numpy as jnp
from jax import lax
from jax.experimental import pallas as pl
from jax.experimental.pallas import tpu as pltpu
from jax.sharding import PartitionSpec as P

normal_levels = (
    -1.0,
    -0.6961928009986877,
    -0.5250730514526367,
    -0.39491748809814453,
    -0.28444138169288635,
    -0.18477343022823334,
    -0.09105003625154495,
    0.0,
    0.07958029955625534,
    0.16093020141124725,
    0.24611230194568634,
    0.33791524171829224,
    0.44070982933044434,
    0.5626170039176941,
    0.7229568362236023,
    1.0,
)
adapter_scale = 2.0
norm_eps = 1e-06
MESH = pl.DeviceIdType.MESH
NB = 7
LANES = 128
f32, bf16 = jnp.float32, jnp.bfloat16


def dot(a, b):
    return jnp.dot(a, b, preferred_element_type=f32)


def dot_nt(a, b):
    return lax.dot_general(a, b, (((1,), (1,)), ((), ())), preferred_element_type=f32)


def dot_tn(a, b):
    return lax.dot_general(a, b, (((0,), (0,)), ((), ())), preferred_element_type=f32)


def nibble_levels(words, shift):
    values = list(normal_levels)
    for bit in range(4):
        mask = jnp.bitwise_and(words, 1 << (shift + bit)) != 0
        values = [
            jnp.where(mask, values[2 * n + 1], values[2 * n]) for n in range(len(values) // 2)
        ]
    return values[0]


def kernel(
    tokens_ref, levels_hbm, scale_ref, down_ref, up_ref, mag_in_ref, grad_hbm,
    tg_ref, dg_ref, ug_ref, mg_ref,
    levels, grads, tok, perm, a_perm, a_own, w, sbuf, own_part, pe_send, pe_recv, pm_send, pm_recv,
    ss_own, ss_e, ss_m_send, ss_m_recv, scaled, mags, mags_in,
    in_x, in_z, in_y, upb,
    ga_send, ga_recv, gb_send, gb_recv, ga2_send, ga2_recv, gb2_send, gb2_recv, gz_keep, gz_send, gz_recv,
    br_x, br_y, br_zh_send, br_zh_recv, br_z, dg_send, dg_recv,
    u_part, u_recv, u_x, u_other,
    local_sem, t_s, t_r, w_s, w_r, f_s, f_r, e_s, e_r, se_s, se_r, m_s, m_r, sm_s, sm_r, c_s, c_r, mg_s, mg_r,
    ix_s, ix_r, iz_s, iz_r, iy_s, iy_r,
    ga_s, ga_r, gb_s, gb_r, ga2_s, ga2_r, gb2_s, gb2_r, gz_s, gz_r,
    bx_s, bx_r, by_s, by_r, bh_s, bh_r, bz_s, bz_r, dg_s, dg_r,
    ud_s, ud_r, ux_s, ux_r, uo_s, uo_r,
):
    dp, row, col = lax.axis_index("dp"), lax.axis_index("row"), lax.axis_index("col")
    z, x = row // 4, row % 4
    y, zh = col // 2, col % 2

    def xpeer(d):
        return {"row": z * 4 + (x + d) % 4}

    def zpeer(d):
        return {"row": ((z + d) % 4) * 4 + x}

    def ypeer(d):
        return {"col": ((y + d) % 4) * 2 + zh}

    zhpeer = {"col": y * 2 + 1 - zh}
    sibling = {"dp": 1 - dp}
    is_mid = (z == 1) | (z == 2)
    is_end = (z == 0) | (z == 3)
    mid_of_end = {"row": jnp.where(z == 0, 1, 2) * 4 + x}
    end_of_mid = {"row": jnp.where(z == 1, 0, 3) * 4 + x}
    other_mid = {"row": jnp.where(z == 1, 2, 1) * 4 + x}

    def rc(src, dst, s, r, dev):
        return pltpu.make_async_remote_copy(
            src_ref=src, dst_ref=dst, send_sem=s, recv_sem=r, device_id=dev, device_id_type=MESH
        )

    lev_copy = pltpu.make_async_copy(levels_hbm.at[dp], levels, local_sem.at[0])
    lev_copy.start()
    grad_copy = pltpu.make_async_copy(
        grad_hbm.at[:, pl.ds(pl.multiple_of(x * (NB * LANES), LANES), NB * LANES)],
        grads, local_sem.at[1],
    )
    grad_copy.start()

    barrier = pltpu.get_barrier_semaphore()
    peers = [xpeer(d) for d in (1, 2, 3)] + [zpeer(d) for d in (1, 2, 3)]
    peers += [ypeer(d) for d in (1, 2, 3)] + [zhpeer, sibling]
    for dev in peers:
        pl.semaphore_signal(barrier, inc=1, device_id=dev, device_id_type=MESH)

    r_id = lax.broadcasted_iota(jnp.int32, (512, 512), 0)
    i_id = lax.broadcasted_iota(jnp.int32, (512, 512), 1)
    at = jnp.where(r_id < 256, 2 * r_id, 2 * r_id - 511)
    perm[...] = jnp.where(i_id == at, 1.0, 0.0).astype(bf16)
    tok[x] = dot_nt(tokens_ref[...], perm[...]).astype(bf16)
    a_full = dot(perm[...], down_ref[...])
    a_perm[...] = a_full.astype(bf16)
    rank_id = lax.broadcasted_iota(jnp.int32, (512, LANES), 1)
    a_own[...] = jnp.where((rank_id >= 64) == (dp == 1), adapter_scale * a_full, 0.0).astype(bf16)
    pl.semaphore_wait(barrier, len(peers))

    for d in (1, 2, 3):
        rc(tok.at[x], tok.at[x], t_s.at[d], t_r.at[x], xpeer(d)).start()

    tok_y = tokens_ref[pl.ds(pl.multiple_of(y * 128, 128), 128), :]
    in_x[x] = dot(tok_y, down_ref[...]).astype(bf16)
    for d in (1, 2, 3):
        rc(in_x.at[x], in_x.at[x], ix_s.at[d], ix_r.at[x], xpeer(d)).start()

    for j in range(NB):
        cols = pl.ds(pl.multiple_of(x * (NB * LANES) + j * LANES, LANES), LANES)
        zero = jnp.zeros((64, LANES), bf16)
        upb[j, 0:64, 0:128] = up_ref[0:64, cols]
        upb[j, 64:128, 128:256] = up_ref[64:128, cols]
        upb[j, 0:64, 128:256] = zero
        upb[j, 64:128, 0:128] = zero
    mags[...] = jnp.zeros_like(mags)
    lev_copy.wait()

    def decode(j, target, store):
        cols = pl.ds(pl.multiple_of((target * NB + j) * LANES, LANES), LANES)
        words = levels[:, cols]
        scales = scale_ref[dp, :, cols]
        for k in range(2):
            lv = nibble_levels(words, 4 * k).reshape(8, 32, LANES)
            base = (lv * scales[:, None, :]).reshape(256, LANES)
            low = dot(a_own[k * 256 : (k + 1) * 256, :], up_ref[:, cols])
            store(k, (base + low).astype(bf16))

    def step(it, carry):
        @pl.when(it < NB)
        def _():
            j = it
            for d in (1, 2, 3):
                def put(k, v, d=d):
                    sbuf[j, d - 1, k * 256 : (k + 1) * 256, :] = v

                decode(j, (x + d) % 4, put)
                rc(sbuf.at[j, d - 1], w.at[j, dp, x], w_s.at[j, d], w_r.at[j, x], xpeer(d)).start()

            def put_own(k, v):
                w[j, dp, x, k * 256 : (k + 1) * 256, :] = v

            decode(j, x, put_own)

        @pl.when(it == 0)
        def _():
            for d in (1, 2, 3):
                src = (x + d) % 4
                rc(tok.at[src], tok.at[src], t_s.at[d], t_r.at[src], xpeer(d)).wait_recv()

        @pl.when(it == 2)
        def _():
            for d in (1, 2, 3):
                src = (x + d) % 4
                rc(in_x.at[src], in_x.at[src], ix_s.at[d], ix_r.at[src], xpeer(d)).wait_recv()
            total = in_x[0].astype(f32) + in_x[1].astype(f32) + in_x[2].astype(f32) + in_x[3].astype(f32)
            in_z[z] = total.astype(bf16)
            for d in (1, 2, 3):
                rc(in_z.at[z], in_z.at[z], iz_s.at[d], iz_r.at[z], zpeer(d)).start()

        @pl.when(it == 4)
        def _():
            for d in (1, 2, 3):
                src = (z + d) % 4
                rc(in_z.at[src], in_z.at[src], iz_s.at[d], iz_r.at[src], zpeer(d)).wait_recv()
            total = in_z[0].astype(f32) + in_z[1].astype(f32) + in_z[2].astype(f32) + in_z[3].astype(f32)
            in_y[y] = total.astype(bf16)
            for d in (1, 2, 3):
                rc(in_y.at[y], in_y.at[y], iy_s.at[d], iy_r.at[y], ypeer(d)).start()

        @pl.when((it >= 2) & (it < NB + 2))
        def _():
            j = it - 2
            for d in (1, 2, 3):
                src = (x + d) % 4
                rc(w.at[j, dp, src], w.at[j, dp, src], w_s.at[j, d], w_r.at[j, src], xpeer(d)).wait_recv()
            rc(w.at[j, dp], w.at[j, dp], f_s.at[j], f_r.at[j], sibling).start()

        @pl.when((it >= 3) & (it < NB + 3))
        def _():
            j = it - 3
            rc(w.at[j, 1 - dp], w.at[j, 1 - dp], f_s.at[j], f_r.at[j], sibling).wait_recv()
            part = None
            ss = None
            for s in range(4):
                both = jnp.concatenate([w[j, 0, s], w[j, 1, s]], axis=1)
                term = dot(tok[s], both)
                part = term if part is None else part + term
                wide = both.astype(f32)
                sq = jnp.sum((wide * wide).reshape(64, 8, 256), axis=0)
                ss = sq if ss is None else ss + sq
            ss_own[j] = ss

            @pl.when(is_end)
            def _():
                pe_send[j] = part.astype(bf16)
                rc(pe_send.at[j], pe_recv.at[j], e_s.at[j], e_r.at[j], mid_of_end).start()
                rc(ss_own.at[j], ss_e.at[j], se_s.at[j], se_r.at[j], mid_of_end).start()

            @pl.when(is_mid)
            def _():
                own_part[j] = part

        @pl.when(is_mid & (it >= 4) & (it < NB + 4))
        def _():
            j = it - 4
            rc(pe_send.at[j], pe_recv.at[j], e_s.at[j], e_r.at[j], end_of_mid).wait_recv()
            rc(ss_own.at[j], ss_e.at[j], se_s.at[j], se_r.at[j], end_of_mid).wait_recv()
            pm_send[j] = (own_part[j] + pe_recv[j].astype(f32)).astype(bf16)
            ss_m_send[j] = ss_own[j] + ss_e[j]
            rc(pm_send.at[j], pm_recv.at[j], m_s.at[j], m_r.at[j], other_mid).start()
            rc(ss_m_send.at[j], ss_m_recv.at[j], sm_s.at[j], sm_r.at[j], other_mid).start()

        @pl.when(it == 5)
        def _():
            grad_copy.wait()

        @pl.when(is_mid & (it >= 5) & (it < NB + 5))
        def _():
            j = it - 5
            rc(pm_send.at[j], pm_recv.at[j], m_s.at[j], m_r.at[j], other_mid).wait_recv()
            rc(ss_m_send.at[j], ss_m_recv.at[j], sm_s.at[j], sm_r.at[j], other_mid).wait_recv()
            squares = jnp.sum(ss_m_send[j] + ss_m_recv[j], axis=0, keepdims=True)
            norm = jnp.sqrt(squares + norm_eps)
            cols = pl.ds(pl.multiple_of(x * (NB * LANES) + j * LANES, LANES), LANES)
            fac_g = mag_in_ref[0:1, cols] / norm[:, 0:128]
            fac_u = mag_in_ref[1:2, cols] / norm[:, 128:256]
            own_cols = pl.ds(pl.multiple_of(j * LANES, LANES), LANES)

            def chunk(n, sums):
                rows = pl.ds(pl.multiple_of(n * 64, 64), 64)
                pre = pm_send[j, rows, :].astype(f32) + pm_recv[j, rows, :].astype(f32)
                pre_g, pre_u = pre[:, 0:128], pre[:, 128:256]
                g, u = pre_g * fac_g, pre_u * fac_u
                s = 1.0 / (1.0 + jnp.exp(-g))
                go = grads[rows, own_cols].astype(f32) * s
                dg = go * u * (1.0 + g * (1.0 - s))
                du = go * g
                scaled[j, rows, 0:128] = (dg * fac_g).astype(bf16)
                scaled[j, rows, 128:256] = (du * fac_u).astype(bf16)
                both = jnp.concatenate([dg * pre_g, du * pre_u], axis=1)
                return sums + jnp.sum(both.reshape(8, 8, 256), axis=0)

            sums = lax.fori_loop(0, 8, chunk, jnp.zeros((8, 256), f32))
            rc(scaled.at[j], scaled.at[j], c_s.at[j], c_r.at[j], end_of_mid).start()
            mags[pl.ds(j, 1), :] = jnp.sum(sums, axis=0, keepdims=True) / norm

        return carry

    lax.fori_loop(0, NB + 5, step, 0)

    @pl.when(is_mid)
    def _():
        rc(mags, mags_in, mg_s.at[0], mg_r.at[0], end_of_mid).start()

    @pl.when(is_end)
    def _():
        def wait_scaled(j, carry):
            rc(scaled.at[j], scaled.at[j], c_s.at[j], c_r.at[j], mid_of_end).wait_recv()
            return carry

        lax.fori_loop(0, NB, wait_scaled, 0)

    def back_block(n, carry):
        target = (x + 1 + n) % 4
        acc = jnp.zeros((512, 512), f32)
        for j in range(NB):
            both = jnp.concatenate([w[j, 0, target], w[j, 1, target]], axis=1)
            acc = acc + dot_nt(scaled[j], both)
        out = acc.astype(bf16).reshape(4, 2, 64, 512)
        ga_send[target] = out[:, 0]
        gb_send[target] = out[:, 1]

        @pl.when(n < 3)
        def _():
            rc(ga_send.at[target], ga_recv.at[x], ga_s.at[n], ga_r.at[x], {"row": z * 4 + target}).start()

        for d in (1, 2, 3):
            there = (y + d) % 4
            rc(gb_send.at[target, there], gb_recv.at[target, y], gb_s.at[target, d],
               gb_r.at[target, y], ypeer(d)).start()
        return carry

    lax.fori_loop(0, 4, back_block, 0)

    z_rows = pl.ds(pl.multiple_of(z * 128, 128), 128)
    back = jnp.zeros((128, LANES), f32)
    for j in range(NB):
        back = back + dot_nt(scaled[j, z_rows, :], upb[j])
    br_x[x] = back.astype(bf16)
    for d in (1, 2, 3):
        rc(br_x.at[x], br_x.at[x], bx_s.at[d], bx_r.at[x], xpeer(d)).start()

    for d in (1, 2, 3):
        src = (y + d) % 4
        rc(in_y.at[src], in_y.at[src], iy_s.at[d], iy_r.at[src], ypeer(d)).wait_recv()

    @pl.when(is_end)
    def _():
        rc(mags, mags_in, mg_s.at[0], mg_r.at[0], mid_of_end).wait_recv()
        mags[...] = mags_in[...]

    inner = in_y[...].reshape(512, LANES)
    for j in range(NB):
        own_cols = slice(j * LANES, (j + 1) * LANES)
        full = adapter_scale * dot_tn(inner, scaled[j])
        u_part[0, 0:64, own_cols] = full[0:64, 0:128]
        u_part[1, 0:64, own_cols] = full[64:128, 128:256]
        for p in range(2):
            u_part[p, 64:72, own_cols] = jnp.broadcast_to(
                mags[j : j + 1, p * 128 : (p + 1) * 128], (8, LANES)
            )
    rc(u_part.at[1 - dp], u_recv, ud_s.at[0], ud_r.at[0], sibling).start()

    for d in (1, 2, 3):
        src = (x + d) % 4
        rc(br_x.at[src], br_x.at[src], bx_s.at[d], bx_r.at[src], xpeer(d)).wait_recv()
    total = br_x[0].astype(f32) + br_x[1].astype(f32) + br_x[2].astype(f32) + br_x[3].astype(f32)
    br_y[y] = total.astype(bf16)
    for d in (1, 2, 3):
        rc(br_y.at[y], br_y.at[y], by_s.at[d], by_r.at[y], ypeer(d)).start()

    rc(u_part.at[1 - dp], u_recv, ud_s.at[0], ud_r.at[0], sibling).wait_recv()
    u_sum = u_part[dp] + u_recv[...]
    u_x[x, 0:72] = u_sum.astype(bf16)
    u_x[x, 72:80] = jnp.zeros((8, NB * LANES), bf16)
    for d in (1, 2, 3):
        rc(u_x.at[x], u_x.at[x], ux_s.at[d], ux_r.at[x], xpeer(d)).start()

    for d in (1, 2, 3):
        src = (y + d) % 4
        rc(br_y.at[src], br_y.at[src], by_s.at[d], by_r.at[src], ypeer(d)).wait_recv()
    total = br_y[0].astype(f32) + br_y[1].astype(f32) + br_y[2].astype(f32) + br_y[3].astype(f32)
    br_zh_send[...] = total.astype(bf16)
    rc(br_zh_send, br_zh_recv, bh_s.at[0], bh_r.at[0], zhpeer).start()

    for d in (1, 2, 3):
        src = (x + d) % 4
        rc(ga_send.at[0], ga_recv.at[src], ga_s.at[0], ga_r.at[src], xpeer(d)).wait_recv()
    acc = ga_send[x].astype(f32)
    for d in (1, 2, 3):
        acc = acc + ga_recv[(x + d) % 4].astype(f32)
    ga2_send[...] = acc.astype(bf16)
    for d in (1, 2, 3):
        rc(ga2_send.at[(y + d) % 4], ga2_recv.at[y], ga2_s.at[d], ga2_r.at[y], ypeer(d)).start()
    for d in (1, 2, 3):
        src = (y + d) % 4
        for t in range(4):
            rc(gb_send.at[t, src], gb_recv.at[t, src], gb_s.at[t, d], gb_r.at[t, src], ypeer(d)).wait_recv()
    for t in range(4):
        acc = gb_send[t, y].astype(f32)
        for d in (1, 2, 3):
            acc = acc + gb_recv[t, (y + d) % 4].astype(f32)
        gb2_send[t] = acc.astype(bf16)
    for d in (1, 2, 3):
        rc(gb2_send.at[(x + d) % 4], gb2_recv.at[x], gb2_s.at[d], gb2_r.at[x], xpeer(d)).start()

    rc(br_zh_send, br_zh_recv, bh_s.at[0], bh_r.at[0], zhpeer).wait_recv()
    br_z[z] = (br_zh_send[...].astype(f32) + br_zh_recv[...].astype(f32)).astype(bf16)
    for d in (1, 2, 3):
        rc(br_z.at[z], br_z.at[z], bz_s.at[d], bz_r.at[z], zpeer(d)).start()

    for d in (1, 2, 3):
        src = (x + d) % 4
        rc(u_x.at[src], u_x.at[src], ux_s.at[d], ux_r.at[src], xpeer(d)).wait_recv()
    rc(u_x, u_other, uo_s.at[0], uo_r.at[0], sibling).start()

    for d in (1, 2, 3):
        src = (y + d) % 4
        rc(ga2_send.at[0], ga2_recv.at[src], ga2_s.at[d], ga2_r.at[src], ypeer(d)).wait_recv()
    acc_a = ga2_send[y].astype(f32)
    for d in (1, 2, 3):
        acc_a = acc_a + ga2_recv[(y + d) % 4].astype(f32)
    for d in (1, 2, 3):
        src = (x + d) % 4
        rc(gb2_send.at[0], gb2_recv.at[src], gb2_s.at[d], gb2_r.at[src], xpeer(d)).wait_recv()
    acc_b = gb2_send[x].astype(f32)
    for d in (1, 2, 3):
        acc_b = acc_b + gb2_recv[(x + d) % 4].astype(f32)
    gz_send[...] = jnp.where(zh == 0, acc_b, acc_a).astype(bf16)
    rc(gz_send, gz_recv, gz_s.at[0], gz_r.at[0], zhpeer).start()
    gz_keep[...] = jnp.where(zh == 0, acc_a, acc_b)

    for d in (1, 2, 3):
        src = (z + d) % 4
        rc(br_z.at[src], br_z.at[src], bz_s.at[d], bz_r.at[src], zpeer(d)).wait_recv()
    dg_send[...] = adapter_scale * dot_tn(tokens_ref[...], br_z[...].reshape(512, LANES))
    rc(dg_send, dg_recv, dg_s.at[0], dg_r.at[0], sibling).start()

    def write_u(p, src_ref):
        for s in range(4):
            lanes = slice(s * NB * LANES, (s + 1) * NB * LANES)
            ug_ref[p, :, lanes] = src_ref[s, 0:64].astype(f32)
            mg_ref[pl.ds(p, 1), lanes] = src_ref[s, 64:80].astype(f32)[0:1]

    write_u(dp, u_x)
    rc(u_x, u_other, uo_s.at[0], uo_r.at[0], sibling).wait_recv()
    write_u(1 - dp, u_other)

    rc(dg_send, dg_recv, dg_s.at[0], dg_r.at[0], sibling).wait_recv()
    dg_ref[...] = dg_send[...] + dg_recv[...]

    rc(gz_send, gz_recv, gz_s.at[0], gz_r.at[0], zhpeer).wait_recv()
    final = (gz_keep[...] + gz_recv[...].astype(f32)).astype(bf16)
    tg_ref[...] = dot(final, perm[...]).astype(bf16)

    for d in (1, 2, 3):
        rc(tok.at[x], tok.at[x], t_s.at[d], t_r.at[x], xpeer(d)).wait_send()
        rc(in_x.at[x], in_x.at[x], ix_s.at[d], ix_r.at[x], xpeer(d)).wait_send()
        rc(in_z.at[z], in_z.at[z], iz_s.at[d], iz_r.at[z], zpeer(d)).wait_send()
        rc(in_y.at[y], in_y.at[y], iy_s.at[d], iy_r.at[y], ypeer(d)).wait_send()
        rc(br_x.at[x], br_x.at[x], bx_s.at[d], bx_r.at[x], xpeer(d)).wait_send()
        rc(br_y.at[y], br_y.at[y], by_s.at[d], by_r.at[y], ypeer(d)).wait_send()
        rc(br_z.at[z], br_z.at[z], bz_s.at[d], bz_r.at[z], zpeer(d)).wait_send()
        rc(u_x.at[x], u_x.at[x], ux_s.at[d], ux_r.at[x], xpeer(d)).wait_send()
        rc(ga_send.at[0], ga_recv.at[0], ga_s.at[d - 1], ga_r.at[0], xpeer(d)).wait_send()
        rc(ga2_send.at[0], ga2_recv.at[0], ga2_s.at[d], ga2_r.at[0], ypeer(d)).wait_send()
        rc(gb2_send.at[0], gb2_recv.at[0], gb2_s.at[d], gb2_r.at[0], xpeer(d)).wait_send()
        for t in range(4):
            rc(gb_send.at[t, 0], gb_recv.at[t, 0], gb_s.at[t, d], gb_r.at[t, 0], ypeer(d)).wait_send()
    rc(br_zh_send, br_zh_recv, bh_s.at[0], bh_r.at[0], zhpeer).wait_send()
    rc(gz_send, gz_recv, gz_s.at[0], gz_r.at[0], zhpeer).wait_send()
    rc(u_part.at[1 - dp], u_recv, ud_s.at[0], ud_r.at[0], sibling).wait_send()
    rc(u_x, u_other, uo_s.at[0], uo_r.at[0], sibling).wait_send()
    rc(dg_send, dg_recv, dg_s.at[0], dg_r.at[0], sibling).wait_send()

    def drain(j, carry):
        for d in (1, 2, 3):
            rc(sbuf.at[j, d - 1], w.at[j, dp, x], w_s.at[j, d], w_r.at[j, x], xpeer(d)).wait_send()
        rc(w.at[j, dp], w.at[j, dp], f_s.at[j], f_r.at[j], sibling).wait_send()

        @pl.when(is_end)
        def _():
            rc(pe_send.at[j], pe_recv.at[j], e_s.at[j], e_r.at[j], mid_of_end).wait_send()
            rc(ss_own.at[j], ss_e.at[j], se_s.at[j], se_r.at[j], mid_of_end).wait_send()

        @pl.when(is_mid)
        def _():
            rc(pm_send.at[j], pm_recv.at[j], m_s.at[j], m_r.at[j], other_mid).wait_send()
            rc(ss_m_send.at[j], ss_m_recv.at[j], sm_s.at[j], sm_r.at[j], other_mid).wait_send()
            rc(scaled.at[j], scaled.at[j], c_s.at[j], c_r.at[j], end_of_mid).wait_send()

        return carry

    lax.fori_loop(0, NB, drain, 0)

    @pl.when(is_mid)
    def _():
        rc(mags, mags_in, mg_s.at[0], mg_r.at[0], end_of_mid).wait_send()


def shards(tokens, levels, scales, down, up, magnitude, grad):
    V = pltpu.VMEM
    D = pltpu.SemaphoreType.DMA
    buffers = [
        V((256, 3584), jnp.int32), V((512, 896), bf16), V((4, 512, 512), bf16), V((512, 512), bf16),
        V((512, 128), bf16), V((512, 128), bf16), V((NB, 2, 4, 512, 128), bf16), V((NB, 3, 512, 128), bf16),
        V((NB, 512, 256), f32), V((NB, 512, 256), bf16), V((NB, 512, 256), bf16),
        V((NB, 512, 256), bf16), V((NB, 512, 256), bf16),
        V((NB, 8, 256), f32), V((NB, 8, 256), f32), V((NB, 8, 256), f32), V((NB, 8, 256), f32),
        V((NB, 512, 256), bf16), V((8, 256), f32), V((8, 256), f32),
        V((4, 128, 128), bf16), V((4, 128, 128), bf16), V((4, 128, 128), bf16), V((NB, 128, 256), bf16),
        V((4, 4, 64, 512), bf16), V((4, 4, 64, 512), bf16), V((4, 4, 64, 512), bf16), V((4, 4, 64, 512), bf16),
        V((4, 64, 512), bf16), V((4, 64, 512), bf16), V((4, 64, 512), bf16), V((4, 64, 512), bf16),
        V((64, 512), f32), V((64, 512), bf16), V((64, 512), bf16),
        V((4, 128, 128), bf16), V((4, 128, 128), bf16), V((128, 128), bf16), V((128, 128), bf16),
        V((4, 128, 128), bf16), V((512, 128), f32), V((512, 128), f32),
        V((2, 72, 896), f32), V((72, 896), f32), V((4, 80, 896), bf16), V((4, 80, 896), bf16),
    ]
    sems = [D((2,)), D((4,)), D((4,)), D((NB, 4)), D((NB, 4))]
    sems += [D((NB,))] * 12 + [D((1,))] * 2
    sems += [D((4,))] * 6
    sems += [D((4,)), D((4,)), D((4, 4)), D((4, 4)), D((4,)), D((4,)), D((4,)), D((4,)), D((1,)), D((1,))]
    sems += [D((4,)), D((4,)), D((4,)), D((4,)), D((1,)), D((1,)), D((4,)), D((4,)), D((1,)), D((1,))]
    sems += [D((1,)), D((1,)), D((4,)), D((4,)), D((1,)), D((1,))]
    vm = pl.BlockSpec(memory_space=pltpu.VMEM)
    hbm = pl.BlockSpec(memory_space=pl.ANY)
    return pl.pallas_call(
        kernel,
        out_shape=(
            jax.ShapeDtypeStruct((64, 512), bf16),
            jax.ShapeDtypeStruct((512, 128), f32),
            jax.ShapeDtypeStruct((2, 64, 3584), f32),
            jax.ShapeDtypeStruct((2, 3584), f32),
        ),
        in_specs=[vm, hbm, vm, vm, vm, vm, hbm],
        out_specs=(vm, vm, vm, vm),
        scratch_shapes=buffers + sems,
        compiler_params=pltpu.CompilerParams(
            collective_id=0, has_side_effects=True, vmem_limit_bytes=56 * 1024 * 1024
        ),
        name="qdora_backward",
    )(tokens, levels, scales, down, up.reshape(128, 3584), magnitude, grad)


def solution(mesh):
    placed = (
        P("dp", "row"),
        P(None, "row", "col"),
        P(None, "row", "col"),
        P("row", None),
        P(None, None, "col"),
        P(None, "col"),
        P("dp", "col"),
    )
    return jax.shard_map(
        shards,
        mesh=mesh,
        in_specs=placed,
        out_specs=(P(("dp", "col"), "row"), P("row", None), P(None, None, "col"), P(None, "col")),
        check_vma=False,
    )
```

```python
import functools

import jax
import jax.numpy as jnp
from jax import lax
from jax.experimental import pallas as pl
from jax.experimental.pallas import tpu as pltpu
from jax.sharding import PartitionSpec as P

normal_levels = (
    -1.0,
    -0.6961928009986877,
    -0.5250730514526367,
    -0.39491748809814453,
    -0.28444138169288635,
    -0.18477343022823334,
    -0.09105003625154495,
    0.0,
    0.07958029955625534,
    0.16093020141124725,
    0.24611230194568634,
    0.33791524171829224,
    0.44070982933044434,
    0.5626170039176941,
    0.7229568362236023,
    1.0,
)
adapter_scale = 2.0
norm_eps = 1e-06
MESH = pl.DeviceIdType.MESH
NB = 7
LANES = 128
LEAD = 4
f32, bf16 = jnp.float32, jnp.bfloat16


def dot(a, b):
    return jnp.dot(a, b, preferred_element_type=f32)


def dot_nt(a, b):
    return lax.dot_general(a, b, (((1,), (1,)), ((), ())), preferred_element_type=f32)


def dot_tn(a, b):
    return lax.dot_general(a, b, (((0,), (0,)), ((), ())), preferred_element_type=f32)


def nibble_levels(words, shift):
    values = list(normal_levels)
    for bit in range(4):
        mask = jnp.bitwise_and(words, 1 << (shift + bit)) != 0
        values = [
            jnp.where(mask, values[2 * n + 1], values[2 * n]) for n in range(len(values) // 2)
        ]
    return values[0]


def kernel(
    tokens_ref, levels_hbm, scale_ref, down_ref, up_ref, mag_in_ref, grad_hbm,
    tg_ref, dg_ref, u_ref,
    levels, grads, tok, perm, a_perm, a_own, w, sbuf, own_part, pe_send, pe_recv, pm_send, pm_recv,
    ss_own, ss_e, ss_m_send, ss_m_recv, scaled, mags, mags_in,
    in_x, in_z, in_y, upb,
    ga_send, ga_recv, gb_send, gb_recv, ga2_send, ga2_recv, gb2_send, gb2_recv, gz_keep, gz_send, gz_recv,
    br_x, br_y, br_zh_send, br_zh_recv, br_z, dg_send, dg_recv,
    u_part, u_recv, u_x, u_other,
    local_sem, t_s, t_r, ty_s, ty_r, w_s, w_r, f_s, f_r, e_s, e_r, se_s, se_r, m_s, m_r, sm_s, sm_r, c_s, c_r, mg_s, mg_r,
    ix_s, ix_r, iz_s, iz_r, iy_s, iy_r,
    ga_s, ga_r, gb_s, gb_r, ga2_s, ga2_r, gb2_s, gb2_r, gz_s, gz_r,
    bx_s, bx_r, by_s, by_r, bh_s, bh_r, bz_s, bz_r, dg_s, dg_r,
    ud_s, ud_r, ux_s, ux_r, uo_s, uo_r,
):
    dp, row, col = lax.axis_index("dp"), lax.axis_index("row"), lax.axis_index("col")
    z, x = row // 4, row % 4
    y, zh = col // 2, col % 2

    def xpeer(d):
        return {"row": z * 4 + (x + d) % 4}

    def zpeer(d):
        return {"row": ((z + d) % 4) * 4 + x}

    def ypeer(d):
        return {"col": ((y + d) % 4) * 2 + zh}

    zhpeer = {"col": y * 2 + 1 - zh}
    sibling = {"dp": 1 - dp}
    is_mid = (z == 1) | (z == 2)
    is_end = (z == 0) | (z == 3)
    mid_of_end = {"row": jnp.where(z == 0, 1, 2) * 4 + x}
    end_of_mid = {"row": jnp.where(z == 1, 0, 3) * 4 + x}
    other_mid = {"row": jnp.where(z == 1, 2, 1) * 4 + x}

    def rc(src, dst, s, r, dev):
        return pltpu.make_async_remote_copy(
            src_ref=src, dst_ref=dst, send_sem=s, recv_sem=r, device_id=dev, device_id_type=MESH
        )

    lev_copy = pltpu.make_async_copy(levels_hbm.at[dp], levels, local_sem.at[0])
    lev_copy.start()
    grad_copy = pltpu.make_async_copy(
        grad_hbm.at[:, pl.ds(pl.multiple_of(x * (NB * LANES), LANES), NB * LANES)],
        grads, local_sem.at[1],
    )
    grad_copy.start()

    barrier = pltpu.get_barrier_semaphore()
    peers = [xpeer(d) for d in (1, 2, 3)] + [zpeer(d) for d in (1, 2, 3)]
    peers += [ypeer(d) for d in (1, 2, 3)] + [zhpeer, sibling]
    for dev in peers:
        pl.semaphore_signal(barrier, inc=1, device_id=dev, device_id_type=MESH)

    r_id = lax.broadcasted_iota(jnp.int32, (512, 512), 0)
    i_id = lax.broadcasted_iota(jnp.int32, (512, 512), 1)
    at = jnp.where(r_id < 256, 2 * r_id, 2 * r_id - 511)
    perm[...] = jnp.where(i_id == at, 1.0, 0.0).astype(bf16)
    own = dot_nt(tokens_ref[...], perm[...]).astype(bf16).reshape(4, 2, 64, 512)
    for h in range(2):
        tok[0, h] = own[:, h]
    a_full = dot(perm[...], down_ref[...])
    a_perm[...] = a_full.astype(bf16)
    rank_id = lax.broadcasted_iota(jnp.int32, (512, LANES), 1)
    a_own[...] = jnp.where((rank_id >= 64) == (dp == 1), adapter_scale * a_full, 0.0).astype(bf16)
    pl.semaphore_wait(barrier, len(peers))

    def token_x(h, d):
        return rc(tok.at[0, h, y], tok.at[4 - d, h, y], t_s.at[h, d], t_r.at[h, 4 - d], xpeer(d))

    def token_y(h, d, q):
        part = tok.at[pl.ds(1, 3), h, q]
        return rc(part, part, ty_s.at[h, d], ty_r.at[h, q], ypeer(d))

    for h in range(2):
        for d in (1, 2, 3):
            token_x(h, d).start()

    tok_y = tokens_ref[pl.ds(pl.multiple_of(y * 128, 128), 128), :]
    in_x[x] = dot(tok_y, down_ref[...]).astype(bf16)
    for d in (1, 2, 3):
        rc(in_x.at[x], in_x.at[x], ix_s.at[d], ix_r.at[x], xpeer(d)).start()

    for j in range(NB):
        cols = pl.ds(pl.multiple_of(x * (NB * LANES) + j * LANES, LANES), LANES)
        zero = jnp.zeros((64, LANES), bf16)
        upb[j, 0:64, 0:128] = up_ref[0:64, cols]
        upb[j, 64:128, 128:256] = up_ref[64:128, cols]
        upb[j, 0:64, 128:256] = zero
        upb[j, 64:128, 0:128] = zero
    mags[...] = jnp.zeros_like(mags)
    lev_copy.wait()

    def decode(j, target, store):
        cols = pl.ds(pl.multiple_of((target * NB + j) * LANES, LANES), LANES)
        words = levels[:, cols]
        scales = scale_ref[dp, :, cols]
        for k in range(2):
            lv = nibble_levels(words, 4 * k).reshape(8, 32, LANES)
            base = (lv * scales[:, None, :]).reshape(256, LANES)
            low = dot(a_own[k * 256 : (k + 1) * 256, :], up_ref[:, cols])
            store(k, (base + low).astype(bf16))

    def weights_x(j, d):
        return rc(sbuf.at[j, d - 1], w.at[j, dp, 4 - d], w_s.at[j, d], w_r.at[j, 4 - d], xpeer(d))

    def step(it, carry):
        @pl.when((it % 2 == 0) & (it < 2 * NB))
        def _():
            j = it // 2
            for d in (1, 2, 3):
                def put(k, v, d=d):
                    sbuf[j, d - 1, k * 256 : (k + 1) * 256, :] = v

                decode(j, (x + d) % 4, put)
                weights_x(j, d).start()

            def put_own(k, v):
                w[j, dp, 0, k * 256 : (k + 1) * 256, :] = v

            decode(j, x, put_own)

        for h in range(2):
            @pl.when(it == 1 + 2 * h)
            def _():
                for d in (1, 2, 3):
                    token_x(h, d).wait_recv()
                for d in (1, 2, 3):
                    token_y(h, d, y).start()

        @pl.when(it == 7)
        def _():
            for d in (1, 2, 3):
                src = (x + d) % 4
                rc(in_x.at[src], in_x.at[src], ix_s.at[d], ix_r.at[src], xpeer(d)).wait_recv()
            total = in_x[0].astype(f32) + in_x[1].astype(f32) + in_x[2].astype(f32) + in_x[3].astype(f32)
            in_z[z] = total.astype(bf16)
            for d in (1, 2, 3):
                rc(in_z.at[z], in_z.at[z], iz_s.at[d], iz_r.at[z], zpeer(d)).start()

        @pl.when(it == 11)
        def _():
            for d in (1, 2, 3):
                src = (z + d) % 4
                rc(in_z.at[src], in_z.at[src], iz_s.at[d], iz_r.at[src], zpeer(d)).wait_recv()
            total = in_z[0].astype(f32) + in_z[1].astype(f32) + in_z[2].astype(f32) + in_z[3].astype(f32)
            in_y[y] = total.astype(bf16)
            for d in (1, 2, 3):
                rc(in_y.at[y], in_y.at[y], iy_s.at[d], iy_r.at[y], ypeer(d)).start()

        @pl.when((it % 2 == 0) & (it >= LEAD) & (it < LEAD + 2 * NB))
        def _():
            j = (it - LEAD) // 2
            for d in (1, 2, 3):
                weights_x(j, d).wait_recv()
            rc(w.at[j, dp], w.at[j, dp], f_s.at[j], f_r.at[j], sibling).start()

        for h in range(2):
            @pl.when(it == LEAD + 2 + h)
            def _():
                for d in (1, 2, 3):
                    token_y(h, d, (y + d) % 4).wait_recv()

        @pl.when((it >= LEAD + 2) & (it < LEAD + 2 + 2 * NB))
        def _():
            unit = it - (LEAD + 2)
            j, h = unit // 2, unit % 2

            @pl.when(h == 0)
            def _():
                rc(w.at[j, 1 - dp], w.at[j, 1 - dp], f_s.at[j], f_r.at[j], sibling).wait_recv()
                ss = None
                for s in range(4):
                    wide = jnp.concatenate([w[j, 0, s], w[j, 1, s]], axis=1).astype(f32)
                    sq = jnp.sum((wide * wide).reshape(64, 8, 256), axis=0)
                    ss = sq if ss is None else ss + sq
                ss_own[j] = ss

                @pl.when(is_end)
                def _():
                    rc(ss_own.at[j], ss_e.at[j], se_s.at[j], se_r.at[j], mid_of_end).start()

            part = None
            for s in range(4):
                both = jnp.concatenate([w[j, 0, s], w[j, 1, s]], axis=1)
                term = dot(tok[s, h].reshape(256, 512), both)
                part = term if part is None else part + term

            @pl.when(is_end)
            def _():
                pe_send[unit] = part.astype(bf16)
                rc(pe_send.at[unit], pe_recv.at[unit], e_s.at[unit], e_r.at[unit], mid_of_end).start()

            @pl.when(is_mid)
            def _():
                own_part[unit] = part

        @pl.when(is_mid & (it >= LEAD + 3) & (it < LEAD + 3 + 2 * NB))
        def _():
            unit = it - (LEAD + 3)
            j, h = unit // 2, unit % 2

            @pl.when(h == 0)
            def _():
                rc(ss_own.at[j], ss_e.at[j], se_s.at[j], se_r.at[j], end_of_mid).wait_recv()
                ss_m_send[j] = ss_own[j] + ss_e[j]
                rc(ss_m_send.at[j], ss_m_recv.at[j], sm_s.at[j], sm_r.at[j], other_mid).start()

            rc(pe_send.at[unit], pe_recv.at[unit], e_s.at[unit], e_r.at[unit], end_of_mid).wait_recv()
            pm_send[unit] = (own_part[unit] + pe_recv[unit].astype(f32)).astype(bf16)
            rc(pm_send.at[unit], pm_recv.at[unit], m_s.at[unit], m_r.at[unit], other_mid).start()

        @pl.when(it == LEAD + 4)
        def _():
            grad_copy.wait()

        @pl.when(is_mid & (it >= LEAD + 4) & (it < LEAD + 4 + 2 * NB))
        def _():
            unit = it - (LEAD + 4)
            j, h = unit // 2, unit % 2

            @pl.when(h == 0)
            def _():
                rc(ss_m_send.at[j], ss_m_recv.at[j], sm_s.at[j], sm_r.at[j], other_mid).wait_recv()

            rc(pm_send.at[unit], pm_recv.at[unit], m_s.at[unit], m_r.at[unit], other_mid).wait_recv()
            squares = jnp.sum(ss_m_send[j] + ss_m_recv[j], axis=0, keepdims=True)
            norm = jnp.sqrt(squares + norm_eps)
            cols = pl.ds(pl.multiple_of(x * (NB * LANES) + j * LANES, LANES), LANES)
            fac_g = mag_in_ref[0:1, cols] / norm[:, 0:128]
            fac_u = mag_in_ref[1:2, cols] / norm[:, 128:256]
            own_cols = pl.ds(pl.multiple_of(j * LANES, LANES), LANES)

            def chunk(n, sums):
                rows = pl.ds(pl.multiple_of(n * 64, 64), 64)
                token_rows = pl.ds(pl.multiple_of(n * 128 + h * 64, 64), 64)
                pre = pm_send[unit, rows, :].astype(f32) + pm_recv[unit, rows, :].astype(f32)
                pre_g, pre_u = pre[:, 0:128], pre[:, 128:256]
                g, u = pre_g * fac_g, pre_u * fac_u
                s = 1.0 / (1.0 + jnp.exp(-g))
                go = grads[token_rows, own_cols].astype(f32) * s
                dg = go * u * (1.0 + g * (1.0 - s))
                du = go * g
                scaled[unit, rows, 0:128] = (dg * fac_g).astype(bf16)
                scaled[unit, rows, 128:256] = (du * fac_u).astype(bf16)
                both = jnp.concatenate([dg * pre_g, du * pre_u], axis=1)
                return sums + jnp.sum(both.reshape(8, 8, 256), axis=0)

            sums = lax.fori_loop(0, 4, chunk, jnp.zeros((8, 256), f32))
            rc(scaled.at[unit], scaled.at[unit], c_s.at[unit], c_r.at[unit], end_of_mid).start()
            mags[pl.ds(unit, 1), :] = jnp.sum(sums, axis=0, keepdims=True) / norm

        return carry

    lax.fori_loop(0, LEAD + 4 + 2 * NB, step, 0)

    @pl.when(is_mid)
    def _():
        rc(mags, mags_in, mg_s.at[0], mg_r.at[0], end_of_mid).start()

    @pl.when(is_end)
    def _():
        def wait_scaled(j, carry):
            rc(scaled.at[j], scaled.at[j], c_s.at[j], c_r.at[j], mid_of_end).wait_recv()
            return carry

        lax.fori_loop(0, 2 * NB, wait_scaled, 0)

    def back_block(n, carry):
        target = (x + 1 + n) % 4
        rel = (1 + n) % 4
        acc = jnp.zeros((512, 512), f32)
        for j in range(NB):
            both = jnp.concatenate([w[j, 0, rel], w[j, 1, rel]], axis=1)
            acc = acc + dot_nt(scaled[2 * j : 2 * j + 2].reshape(512, 256), both)
        out = acc.astype(bf16).reshape(2, 4, 64, 512)
        ga_send[target] = out[0]
        gb_send[target] = out[1]

        @pl.when(n < 3)
        def _():
            rc(ga_send.at[target], ga_recv.at[x], ga_s.at[n], ga_r.at[x], {"row": z * 4 + target}).start()

        for d in (1, 2, 3):
            there = (y + d) % 4
            rc(gb_send.at[target, there], gb_recv.at[target, y], gb_s.at[target, d],
               gb_r.at[target, y], ypeer(d)).start()
        return carry

    lax.fori_loop(0, 4, back_block, 0)

    z_rows = pl.ds(pl.multiple_of(z * 64, 64), 64)
    back = jnp.zeros((128, LANES), f32)
    for j in range(NB):
        back = back + dot_nt(scaled[2 * j : 2 * j + 2, z_rows, :].reshape(128, 256), upb[j])
    br_x[x] = back.astype(bf16)
    for d in (1, 2, 3):
        rc(br_x.at[x], br_x.at[x], bx_s.at[d], bx_r.at[x], xpeer(d)).start()

    for d in (1, 2, 3):
        src = (y + d) % 4
        rc(in_y.at[src], in_y.at[src], iy_s.at[d], iy_r.at[src], ypeer(d)).wait_recv()

    @pl.when(is_end)
    def _():
        rc(mags, mags_in, mg_s.at[0], mg_r.at[0], mid_of_end).wait_recv()
        mags[...] = mags_in[...]

    inner = jnp.concatenate(
        [in_y[...].reshape(4, 2, 64, LANES)[:, h].reshape(256, LANES) for h in range(2)], axis=0
    )
    for j in range(NB):
        own_cols = slice(j * LANES, (j + 1) * LANES)
        full = adapter_scale * dot_tn(inner, scaled[2 * j : 2 * j + 2].reshape(512, 256))
        u_part[0, 0:64, own_cols] = full[0:64, 0:128]
        u_part[1, 0:64, own_cols] = full[64:128, 128:256]
        for p in range(2):
            u_part[p, 64:72, own_cols] = jnp.broadcast_to(
                mags[2 * j : 2 * j + 1, p * 128 : (p + 1) * 128]
                + mags[2 * j + 1 : 2 * j + 2, p * 128 : (p + 1) * 128],
                (8, LANES),
            )
    rc(u_part.at[1 - dp], u_recv, ud_s.at[0], ud_r.at[0], sibling).start()

    for d in (1, 2, 3):
        src = (x + d) % 4
        rc(br_x.at[src], br_x.at[src], bx_s.at[d], bx_r.at[src], xpeer(d)).wait_recv()
    total = br_x[0].astype(f32) + br_x[1].astype(f32) + br_x[2].astype(f32) + br_x[3].astype(f32)
    br_y[y] = total.astype(bf16)
    for d in (1, 2, 3):
        rc(br_y.at[y], br_y.at[y], by_s.at[d], by_r.at[y], ypeer(d)).start()

    rc(u_part.at[1 - dp], u_recv, ud_s.at[0], ud_r.at[0], sibling).wait_recv()
    u_sum = u_part[dp] + u_recv[...]
    u_x[x, 0:72] = u_sum.astype(bf16)
    u_x[x, 72:80] = jnp.zeros((8, NB * LANES), bf16)
    for d in (1, 2, 3):
        rc(u_x.at[x], u_x.at[x], ux_s.at[d], ux_r.at[x], xpeer(d)).start()

    for d in (1, 2, 3):
        src = (y + d) % 4
        rc(br_y.at[src], br_y.at[src], by_s.at[d], by_r.at[src], ypeer(d)).wait_recv()
    total = br_y[0].astype(f32) + br_y[1].astype(f32) + br_y[2].astype(f32) + br_y[3].astype(f32)
    br_zh_send[...] = total.astype(bf16)
    rc(br_zh_send, br_zh_recv, bh_s.at[0], bh_r.at[0], zhpeer).start()

    for d in (1, 2, 3):
        src = (x + d) % 4
        rc(ga_send.at[0], ga_recv.at[src], ga_s.at[0], ga_r.at[src], xpeer(d)).wait_recv()
    acc = ga_send[x].astype(f32)
    for d in (1, 2, 3):
        acc = acc + ga_recv[(x + d) % 4].astype(f32)
    ga2_send[...] = acc.astype(bf16)
    for d in (1, 2, 3):
        rc(ga2_send.at[(y + d) % 4], ga2_recv.at[y], ga2_s.at[d], ga2_r.at[y], ypeer(d)).start()
    for d in (1, 2, 3):
        src = (y + d) % 4
        for t in range(4):
            rc(gb_send.at[t, src], gb_recv.at[t, src], gb_s.at[t, d], gb_r.at[t, src], ypeer(d)).wait_recv()
    for t in range(4):
        acc = gb_send[t, y].astype(f32)
        for d in (1, 2, 3):
            acc = acc + gb_recv[t, (y + d) % 4].astype(f32)
        gb2_send[t] = acc.astype(bf16)
    for d in (1, 2, 3):
        rc(gb2_send.at[(x + d) % 4], gb2_recv.at[x], gb2_s.at[d], gb2_r.at[x], xpeer(d)).start()

    rc(br_zh_send, br_zh_recv, bh_s.at[0], bh_r.at[0], zhpeer).wait_recv()
    br_z[z] = (br_zh_send[...].astype(f32) + br_zh_recv[...].astype(f32)).astype(bf16)
    for d in (1, 2, 3):
        rc(br_z.at[z], br_z.at[z], bz_s.at[d], bz_r.at[z], zpeer(d)).start()

    for d in (1, 2, 3):
        src = (x + d) % 4
        rc(u_x.at[src], u_x.at[src], ux_s.at[d], ux_r.at[src], xpeer(d)).wait_recv()
    rc(u_x, u_other, uo_s.at[0], uo_r.at[0], sibling).start()

    for d in (1, 2, 3):
        src = (y + d) % 4
        rc(ga2_send.at[0], ga2_recv.at[src], ga2_s.at[d], ga2_r.at[src], ypeer(d)).wait_recv()
    acc_a = ga2_send[y].astype(f32)
    for d in (1, 2, 3):
        acc_a = acc_a + ga2_recv[(y + d) % 4].astype(f32)
    for d in (1, 2, 3):
        src = (x + d) % 4
        rc(gb2_send.at[0], gb2_recv.at[src], gb2_s.at[d], gb2_r.at[src], xpeer(d)).wait_recv()
    acc_b = gb2_send[x].astype(f32)
    for d in (1, 2, 3):
        acc_b = acc_b + gb2_recv[(x + d) % 4].astype(f32)
    gz_send[...] = jnp.where(zh == 0, acc_b, acc_a).astype(bf16)
    rc(gz_send, gz_recv, gz_s.at[0], gz_r.at[0], zhpeer).start()
    gz_keep[...] = jnp.where(zh == 0, acc_a, acc_b)

    for d in (1, 2, 3):
        src = (z + d) % 4
        rc(br_z.at[src], br_z.at[src], bz_s.at[d], bz_r.at[src], zpeer(d)).wait_recv()
    dg_send[...] = adapter_scale * dot_tn(tokens_ref[...], br_z[...].reshape(512, LANES))
    rc(dg_send, dg_recv, dg_s.at[0], dg_r.at[0], sibling).start()

    u_ref[dp] = u_x[...]
    rc(u_x, u_other, uo_s.at[0], uo_r.at[0], sibling).wait_recv()
    u_ref[1 - dp] = u_other[...]

    rc(dg_send, dg_recv, dg_s.at[0], dg_r.at[0], sibling).wait_recv()
    dg_ref[...] = dg_send[...] + dg_recv[...]

    rc(gz_send, gz_recv, gz_s.at[0], gz_r.at[0], zhpeer).wait_recv()
    final = (gz_keep[...] + gz_recv[...].astype(f32)).astype(bf16)
    tg_ref[...] = dot(final, perm[...]).astype(bf16)

    for d in (1, 2, 3):
        for h in range(2):
            token_x(h, d).wait_send()
            token_y(h, d, y).wait_send()
        rc(in_x.at[x], in_x.at[x], ix_s.at[d], ix_r.at[x], xpeer(d)).wait_send()
        rc(in_z.at[z], in_z.at[z], iz_s.at[d], iz_r.at[z], zpeer(d)).wait_send()
        rc(in_y.at[y], in_y.at[y], iy_s.at[d], iy_r.at[y], ypeer(d)).wait_send()
        rc(br_x.at[x], br_x.at[x], bx_s.at[d], bx_r.at[x], xpeer(d)).wait_send()
        rc(br_y.at[y], br_y.at[y], by_s.at[d], by_r.at[y], ypeer(d)).wait_send()
        rc(br_z.at[z], br_z.at[z], bz_s.at[d], bz_r.at[z], zpeer(d)).wait_send()
        rc(u_x.at[x], u_x.at[x], ux_s.at[d], ux_r.at[x], xpeer(d)).wait_send()
        rc(ga_send.at[0], ga_recv.at[0], ga_s.at[d - 1], ga_r.at[0], xpeer(d)).wait_send()
        rc(ga2_send.at[0], ga2_recv.at[0], ga2_s.at[d], ga2_r.at[0], ypeer(d)).wait_send()
        rc(gb2_send.at[0], gb2_recv.at[0], gb2_s.at[d], gb2_r.at[0], xpeer(d)).wait_send()
        for t in range(4):
            rc(gb_send.at[t, 0], gb_recv.at[t, 0], gb_s.at[t, d], gb_r.at[t, 0], ypeer(d)).wait_send()
    rc(br_zh_send, br_zh_recv, bh_s.at[0], bh_r.at[0], zhpeer).wait_send()
    rc(gz_send, gz_recv, gz_s.at[0], gz_r.at[0], zhpeer).wait_send()
    rc(u_part.at[1 - dp], u_recv, ud_s.at[0], ud_r.at[0], sibling).wait_send()
    rc(u_x, u_other, uo_s.at[0], uo_r.at[0], sibling).wait_send()
    rc(dg_send, dg_recv, dg_s.at[0], dg_r.at[0], sibling).wait_send()

    def drain(j, carry):
        for d in (1, 2, 3):
            weights_x(j, d).wait_send()
        rc(w.at[j, dp], w.at[j, dp], f_s.at[j], f_r.at[j], sibling).wait_send()

        @pl.when(is_end)
        def _():
            rc(ss_own.at[j], ss_e.at[j], se_s.at[j], se_r.at[j], mid_of_end).wait_send()

        @pl.when(is_mid)
        def _():
            rc(ss_m_send.at[j], ss_m_recv.at[j], sm_s.at[j], sm_r.at[j], other_mid).wait_send()

        return carry

    def drain_unit(unit, carry):
        @pl.when(is_end)
        def _():
            rc(pe_send.at[unit], pe_recv.at[unit], e_s.at[unit], e_r.at[unit], mid_of_end).wait_send()

        @pl.when(is_mid)
        def _():
            rc(pm_send.at[unit], pm_recv.at[unit], m_s.at[unit], m_r.at[unit], other_mid).wait_send()
            rc(scaled.at[unit], scaled.at[unit], c_s.at[unit], c_r.at[unit], end_of_mid).wait_send()

        return carry

    lax.fori_loop(0, 2 * NB, drain_unit, 0)
    lax.fori_loop(0, NB, drain, 0)

    @pl.when(is_mid)
    def _():
        rc(mags, mags_in, mg_s.at[0], mg_r.at[0], end_of_mid).wait_send()


def finish(tg_in, dg_in, u_in, tg_ref, dg_ref, ug_ref, mg_ref):
    tg_ref[...] = tg_in[...]
    dg_ref[...] = dg_in[...]
    for p in range(2):
        for s in range(4):
            lanes = slice(s * NB * LANES, (s + 1) * NB * LANES)
            ug_ref[p, :, lanes] = u_in[p, s, 0:64].astype(f32)
            mg_ref[p : p + 1, lanes] = u_in[p, s, 64:80].astype(f32)[0:1]


def shards(tokens, levels, scales, down, up, magnitude, grad):
    V = pltpu.VMEM
    D = pltpu.SemaphoreType.DMA
    NU = 2 * NB
    buffers = [
        V((256, 3584), jnp.int32), V((512, 896), bf16), V((4, 2, 4, 64, 512), bf16), V((512, 512), bf16),
        V((512, 128), bf16), V((512, 128), bf16), V((NB, 2, 4, 512, 128), bf16), V((NB, 3, 512, 128), bf16),
        V((NU, 256, 256), f32), V((NU, 256, 256), bf16), V((NU, 256, 256), bf16),
        V((NU, 256, 256), bf16), V((NU, 256, 256), bf16),
        V((NB, 8, 256), f32), V((NB, 8, 256), f32), V((NB, 8, 256), f32), V((NB, 8, 256), f32),
        V((NU, 256, 256), bf16), V((16, 256), f32), V((16, 256), f32),
        V((4, 128, 128), bf16), V((4, 128, 128), bf16), V((4, 128, 128), bf16), V((NB, 128, 256), bf16),
        V((4, 4, 64, 512), bf16), V((4, 4, 64, 512), bf16), V((4, 4, 64, 512), bf16), V((4, 4, 64, 512), bf16),
        V((4, 64, 512), bf16), V((4, 64, 512), bf16), V((4, 64, 512), bf16), V((4, 64, 512), bf16),
        V((64, 512), f32), V((64, 512), bf16), V((64, 512), bf16),
        V((4, 128, 128), bf16), V((4, 128, 128), bf16), V((128, 128), bf16), V((128, 128), bf16),
        V((4, 128, 128), bf16), V((512, 128), f32), V((512, 128), f32),
        V((2, 72, 896), f32), V((72, 896), f32), V((4, 80, 896), bf16), V((4, 80, 896), bf16),
    ]
    sems = [D((2,)), D((2, 4)), D((2, 4)), D((2, 4)), D((2, 4)), D((NB, 4)), D((NB, 4))]
    sems += [D((NB,)), D((NB,)), D((NU,)), D((NU,)), D((NB,)), D((NB,))]
    sems += [D((NU,)), D((NU,)), D((NB,)), D((NB,)), D((NU,)), D((NU,)), D((1,)), D((1,))]
    sems += [D((4,))] * 6
    sems += [D((4,)), D((4,)), D((4, 4)), D((4, 4)), D((4,)), D((4,)), D((4,)), D((4,)), D((1,)), D((1,))]
    sems += [D((4,)), D((4,)), D((4,)), D((4,)), D((1,)), D((1,)), D((4,)), D((4,)), D((1,)), D((1,))]
    sems += [D((1,)), D((1,)), D((4,)), D((4,)), D((1,)), D((1,))]
    vm = pl.BlockSpec(memory_space=pltpu.VMEM)
    hbm = pl.BlockSpec(memory_space=pl.ANY)
    token_out, down_out, up_out = pl.pallas_call(
        kernel,
        out_shape=(
            jax.ShapeDtypeStruct((64, 512), bf16),
            jax.ShapeDtypeStruct((512, 128), f32),
            jax.ShapeDtypeStruct((2, 4, 80, 896), bf16),
        ),
        in_specs=[vm, hbm, vm, vm, vm, vm, hbm],
        out_specs=(vm, vm, vm),
        scratch_shapes=buffers + sems,
        compiler_params=pltpu.CompilerParams(
            collective_id=0, has_side_effects=True, vmem_limit_bytes=56 * 1024 * 1024
        ),
        name="qdora_backward",
    )(tokens, levels, scales, down, up.reshape(128, 3584), magnitude, grad)
    return pl.pallas_call(
        finish,
        out_shape=(
            jax.ShapeDtypeStruct((64, 512), bf16),
            jax.ShapeDtypeStruct((512, 128), f32),
            jax.ShapeDtypeStruct((2, 64, 3584), f32),
            jax.ShapeDtypeStruct((2, 3584), f32),
        ),
        in_specs=[vm] * 3,
        out_specs=(vm,) * 4,
        name="write_outputs",
    )(token_out, down_out, up_out)


def solution(mesh):
    placed = (
        P("dp", "row"),
        P(None, "row", "col"),
        P(None, "row", "col"),
        P("row", None),
        P(None, None, "col"),
        P(None, "col"),
        P("dp", "col"),
    )
    return jax.shard_map(
        shards,
        mesh=mesh,
        in_specs=placed,
        out_specs=(P(("dp", "col"), "row"), P("row", None), P(None, None, "col"), P(None, "col")),
        check_vma=False,
    )
```

```python
import functools

import jax
import jax.numpy as jnp
from jax import lax
from jax.experimental import pallas as pl
from jax.experimental.pallas import tpu as pltpu
from jax.sharding import PartitionSpec as P

normal_levels = (
    -1.0,
    -0.6961928009986877,
    -0.5250730514526367,
    -0.39491748809814453,
    -0.28444138169288635,
    -0.18477343022823334,
    -0.09105003625154495,
    0.0,
    0.07958029955625534,
    0.16093020141124725,
    0.24611230194568634,
    0.33791524171829224,
    0.44070982933044434,
    0.5626170039176941,
    0.7229568362236023,
    1.0,
)
adapter_scale = 2.0
norm_eps = 1e-06
MESH = pl.DeviceIdType.MESH
NB = 7
LANES = 128
LEAD = 4
PRE = LEAD + 2
MIX = PRE + 2
GRAD = MIX + 2
f32, bf16 = jnp.float32, jnp.bfloat16


def dot(a, b):
    return jnp.dot(a, b, preferred_element_type=f32)


def dot_nt(a, b):
    return lax.dot_general(a, b, (((1,), (1,)), ((), ())), preferred_element_type=f32)


def dot_tn(a, b):
    return lax.dot_general(a, b, (((0,), (0,)), ((), ())), preferred_element_type=f32)


def nibble_levels(words, shift):
    values = list(normal_levels)
    for bit in range(4):
        mask = jnp.bitwise_and(words, 1 << (shift + bit)) != 0
        values = [
            jnp.where(mask, values[2 * n + 1], values[2 * n]) for n in range(len(values) // 2)
        ]
    return values[0]


def kernel(
    tokens_ref, levels_hbm, scale_ref, down_ref, up_ref, mag_in_ref, grad_hbm,
    tg_ref, dg_ref, u_ref,
    levels, grads, tok, perm, a_perm, a_own, w, sbuf, own_part, pe_send, pe_recv, pm_send, pm_recv,
    ss_own, ss_e, ss_m_send, ss_m_recv, scaled, mags, mags_in,
    in_x, in_z, in_y, upb,
    ga_send, ga_recv, gb_send, gb_recv, ga2_send, ga2_recv, gb2_send, gb2_recv, gz_keep, gz_send, gz_recv,
    br_x, br_y, br_zh_send, br_zh_recv, br_z, dg_send, dg_recv,
    u_part, u_recv, u_x, u_other, inner, token_sum, rank_sum, br_all,
    local_sem, t_s, t_r, ty_s, ty_r, w_s, w_r, f_s, f_r, e_s, e_r, se_s, se_r, m_s, m_r, sm_s, sm_r, c_s, c_r, mg_s, mg_r,
    ix_s, ix_r, iz_s, iz_r, iy_s, iy_r,
    ga_s, ga_r, gb_s, gb_r, ga2_s, ga2_r, gb2_s, gb2_r, gz_s, gz_r,
    bx_s, bx_r, by_s, by_r, bh_s, bh_r, bz_s, bz_r, dg_s, dg_r,
    ud_s, ud_r, ux_s, ux_r, uo_s, uo_r,
):
    dp, row, col = lax.axis_index("dp"), lax.axis_index("row"), lax.axis_index("col")
    z, x = row // 4, row % 4
    y, zh = col // 2, col % 2

    def xpeer(d):
        return {"row": z * 4 + (x + d) % 4}

    def zpeer(d):
        return {"row": ((z + d) % 4) * 4 + x}

    def ypeer(d):
        return {"col": ((y + d) % 4) * 2 + zh}

    zhpeer = {"col": y * 2 + 1 - zh}
    sibling = {"dp": 1 - dp}
    is_mid = (z == 1) | (z == 2)
    is_end = (z == 0) | (z == 3)
    mid_of_end = {"row": jnp.where(z == 0, 1, 2) * 4 + x}
    end_of_mid = {"row": jnp.where(z == 1, 0, 3) * 4 + x}
    other_mid = {"row": jnp.where(z == 1, 2, 1) * 4 + x}

    def rc(src, dst, s, r, dev):
        return pltpu.make_async_remote_copy(
            src_ref=src, dst_ref=dst, send_sem=s, recv_sem=r, device_id=dev, device_id_type=MESH
        )

    lev_copy = pltpu.make_async_copy(levels_hbm.at[dp], levels, local_sem.at[0])
    lev_copy.start()
    grad_copy = pltpu.make_async_copy(
        grad_hbm.at[:, pl.ds(pl.multiple_of(x * (NB * LANES), LANES), NB * LANES)],
        grads, local_sem.at[1],
    )
    grad_copy.start()

    barrier = pltpu.get_barrier_semaphore()
    peers = [xpeer(d) for d in (1, 2, 3)] + [zpeer(d) for d in (1, 2, 3)]
    peers += [ypeer(d) for d in (1, 2, 3)] + [zhpeer, sibling]
    for dev in peers:
        pl.semaphore_signal(barrier, inc=1, device_id=dev, device_id_type=MESH)

    r_id = lax.broadcasted_iota(jnp.int32, (512, 512), 0)
    i_id = lax.broadcasted_iota(jnp.int32, (512, 512), 1)
    at = jnp.where(r_id < 256, 2 * r_id, 2 * r_id - 511)
    perm[...] = jnp.where(i_id == at, 1.0, 0.0).astype(bf16)
    own = dot_nt(tokens_ref[...], perm[...]).astype(bf16).reshape(4, 2, 2, 32, 512)
    for h in range(2):
        tok[0, h] = own[:, :, h].reshape(4, 64, 512)
    a_full = dot(perm[...], down_ref[...])
    a_perm[...] = a_full.astype(bf16)
    rank_id = lax.broadcasted_iota(jnp.int32, (512, LANES), 1)
    a_own[...] = jnp.where((rank_id >= 64) == (dp == 1), adapter_scale * a_full, 0.0).astype(bf16)
    pl.semaphore_wait(barrier, len(peers))

    def token_x(h, d):
        return rc(tok.at[0, h, y], tok.at[4 - d, h, y], t_s.at[h, d], t_r.at[h, 4 - d], xpeer(d))

    def token_y(h, d, q):
        part = tok.at[pl.ds(1, 3), h, q]
        return rc(part, part, ty_s.at[h, d], ty_r.at[h, q], ypeer(d))

    for d in (1, 2, 3):
        token_x(0, d).start()

    tok_y = tokens_ref[pl.ds(pl.multiple_of(y * 128, 128), 128), :]
    in_x[x] = dot(tok_y, down_ref[...]).astype(bf16)
    for d in (1, 2, 3):
        rc(in_x.at[x], in_x.at[x], ix_s.at[d], ix_r.at[x], xpeer(d)).start()

    for j in range(NB):
        cols = pl.ds(pl.multiple_of(x * (NB * LANES) + j * LANES, LANES), LANES)
        zero = jnp.zeros((64, LANES), bf16)
        upb[j, 0:64, 0:128] = up_ref[0:64, cols]
        upb[j, 64:128, 128:256] = up_ref[64:128, cols]
        upb[j, 0:64, 128:256] = zero
        upb[j, 64:128, 0:128] = zero
    mags[...] = jnp.zeros_like(mags)
    lev_copy.wait()

    def decode(j, target, store):
        cols = pl.ds(pl.multiple_of((target * NB + j) * LANES, LANES), LANES)
        words = levels[:, cols]
        scales = scale_ref[dp, :, cols]
        for k in range(2):
            lv = nibble_levels(words, 4 * k).reshape(8, 32, LANES)
            base = (lv * scales[:, None, :]).reshape(256, LANES)
            low = dot(a_own[k * 256 : (k + 1) * 256, :], up_ref[:, cols])
            store(k, (base + low).astype(bf16))

    def weights_x(j, d):
        return rc(sbuf.at[j, d - 1], w.at[j, dp, 4 - d], w_s.at[j, d], w_r.at[j, 4 - d], xpeer(d))

    def place(turn):
        odd = turn % 2 == 1
        j = jnp.where(odd, (turn + 1) // 2, (turn - 2) // 2)
        h = jnp.where(odd, 0, 1)
        j = jnp.where(turn < 5, turn - 3, jnp.where(turn == 2 * NB - 1, NB - 1, j))
        h = jnp.where((turn < 5) | (turn == 2 * NB - 1), 1, h)
        j = jnp.where(turn < 3, turn, j)
        h = jnp.where(turn < 3, 0, h)
        return j, h, 2 * j + h

    z_rows = pl.ds(pl.multiple_of(z * 64, 64), 64)

    def token_terms(h, rel, blocks):
        acc = None
        for j in blocks:
            both = jnp.concatenate([w[j, 0, rel], w[j, 1, rel]], axis=1)
            term = dot_nt(scaled[2 * j + h], both)
            acc = term if acc is None else acc + term
        return acc

    def rank_terms(h, blocks):
        acc = None
        for j in blocks:
            term = dot_nt(scaled[2 * j + h, z_rows, :], upb[j])
            acc = term if acc is None else acc + term
        return acc

    def up_term(j):
        own_cols = slice(j * LANES, (j + 1) * LANES)
        full = dot_tn(inner[0], scaled[2 * j]) + dot_tn(inner[1], scaled[2 * j + 1])
        u_part[0, 0:64, own_cols] = adapter_scale * full[0:64, 0:128]
        u_part[1, 0:64, own_cols] = adapter_scale * full[64:128, 128:256]

    def wait_scaled(unit, carry):
        rc(scaled.at[unit], scaled.at[unit], c_s.at[unit], c_r.at[unit], mid_of_end).wait_recv()
        return carry

    def step(it, carry):
        @pl.when((it % 2 == 0) & (it < 2 * NB))
        def _():
            j = it // 2
            for d in (1, 2, 3):
                def put(k, v, d=d):
                    sbuf[j, d - 1, k * 256 : (k + 1) * 256, :] = v

                decode(j, (x + d) % 4, put)
                weights_x(j, d).start()

            def put_own(k, v):
                w[j, dp, 0, k * 256 : (k + 1) * 256, :] = v

            decode(j, x, put_own)

        @pl.when(it == 1)
        def _():
            for d in (1, 2, 3):
                token_x(1, d).start()
            for d in (1, 2, 3):
                token_x(0, d).wait_recv()
            for d in (1, 2, 3):
                token_y(0, d, y).start()

        @pl.when(it == 7)
        def _():
            for d in (1, 2, 3):
                src = (x + d) % 4
                rc(in_x.at[src], in_x.at[src], ix_s.at[d], ix_r.at[src], xpeer(d)).wait_recv()
            total = in_x[0].astype(f32) + in_x[1].astype(f32) + in_x[2].astype(f32) + in_x[3].astype(f32)
            in_z[z] = total.astype(bf16)
            for d in (1, 2, 3):
                rc(in_z.at[z], in_z.at[z], iz_s.at[d], iz_r.at[z], zpeer(d)).start()

        @pl.when(it == 11)
        def _():
            for d in (1, 2, 3):
                src = (z + d) % 4
                rc(in_z.at[src], in_z.at[src], iz_s.at[d], iz_r.at[src], zpeer(d)).wait_recv()
            total = in_z[0].astype(f32) + in_z[1].astype(f32) + in_z[2].astype(f32) + in_z[3].astype(f32)
            in_y[y] = total.astype(bf16)
            for d in (1, 2, 3):
                rc(in_y.at[y], in_y.at[y], iy_s.at[d], iy_r.at[y], ypeer(d)).start()

        early = (it >= PRE - 1) & (it < PRE + 2)
        late = (it % 2 == 0) & (it >= LEAD + 6) & (it < LEAD + 2 * NB)

        @pl.when(early | late)
        def _():
            j = jnp.where(early, it - (PRE - 1), (it - LEAD) // 2)
            for d in (1, 2, 3):
                weights_x(j, d).wait_recv()
            rc(w.at[j, dp], w.at[j, dp], f_s.at[j], f_r.at[j], sibling).start()

        @pl.when(it == PRE)
        def _():
            for d in (1, 2, 3):
                token_x(1, d).wait_recv()
            for d in (1, 2, 3):
                token_y(0, d, (y + d) % 4).wait_recv()
            for d in (1, 2, 3):
                token_y(1, d, y).start()

        @pl.when(it == PRE + 3)
        def _():
            for d in (1, 2, 3):
                token_y(1, d, (y + d) % 4).wait_recv()

        @pl.when((it >= PRE) & (it < PRE + 2 * NB))
        def _():
            j, h, unit = place(it - PRE)

            @pl.when(h == 0)
            def _():
                rc(w.at[j, 1 - dp], w.at[j, 1 - dp], f_s.at[j], f_r.at[j], sibling).wait_recv()
                ss = None
                for s in range(4):
                    wide = jnp.concatenate([w[j, 0, s], w[j, 1, s]], axis=1).astype(f32)
                    sq = jnp.sum((wide * wide).reshape(64, 8, 256), axis=0)
                    ss = sq if ss is None else ss + sq
                ss_own[j] = ss

                @pl.when(is_end)
                def _():
                    rc(ss_own.at[j], ss_e.at[j], se_s.at[j], se_r.at[j], mid_of_end).start()

            part = None
            for s in range(4):
                both = jnp.concatenate([w[j, 0, s], w[j, 1, s]], axis=1)
                term = dot(tok[s, h].reshape(256, 512), both)
                part = term if part is None else part + term

            @pl.when(is_end)
            def _():
                pe_send[unit] = part.astype(bf16)
                rc(pe_send.at[unit], pe_recv.at[unit], e_s.at[unit], e_r.at[unit], mid_of_end).start()

            @pl.when(is_mid)
            def _():
                own_part[unit] = part

        @pl.when(is_mid & (it >= MIX) & (it < MIX + 2 * NB))
        def _():
            j, h, unit = place(it - MIX)

            @pl.when(h == 0)
            def _():
                rc(ss_own.at[j], ss_e.at[j], se_s.at[j], se_r.at[j], end_of_mid).wait_recv()
                ss_m_send[j] = ss_own[j] + ss_e[j]
                rc(ss_m_send.at[j], ss_m_recv.at[j], sm_s.at[j], sm_r.at[j], other_mid).start()

            rc(pe_send.at[unit], pe_recv.at[unit], e_s.at[unit], e_r.at[unit], end_of_mid).wait_recv()
            pm_send[unit] = (own_part[unit] + pe_recv[unit].astype(f32)).astype(bf16)
            rc(pm_send.at[unit], pm_recv.at[unit], m_s.at[unit], m_r.at[unit], other_mid).start()

        @pl.when(it == GRAD)
        def _():
            grad_copy.wait()

        @pl.when(is_mid & (it >= GRAD) & (it < GRAD + 2 * NB))
        def _():
            j, h, unit = place(it - GRAD)

            @pl.when(h == 0)
            def _():
                rc(ss_m_send.at[j], ss_m_recv.at[j], sm_s.at[j], sm_r.at[j], other_mid).wait_recv()

            rc(pm_send.at[unit], pm_recv.at[unit], m_s.at[unit], m_r.at[unit], other_mid).wait_recv()
            squares = jnp.sum(ss_m_send[j] + ss_m_recv[j], axis=0, keepdims=True)
            norm = jnp.sqrt(squares + norm_eps)
            cols = pl.ds(pl.multiple_of(x * (NB * LANES) + j * LANES, LANES), LANES)
            fac_g = mag_in_ref[0:1, cols] / norm[:, 0:128]
            fac_u = mag_in_ref[1:2, cols] / norm[:, 128:256]
            own_cols = pl.ds(pl.multiple_of(j * LANES, LANES), LANES)

            def chunk(n, sums):
                rows = pl.ds(pl.multiple_of(n * 64, 64), 64)
                token_rows = [pl.ds(pl.multiple_of(n * 128 + q * 64 + h * 32, 32), 32) for q in range(2)]
                pre = pm_send[unit, rows, :].astype(f32) + pm_recv[unit, rows, :].astype(f32)
                pre_g, pre_u = pre[:, 0:128], pre[:, 128:256]
                g, u = pre_g * fac_g, pre_u * fac_u
                s = 1.0 / (1.0 + jnp.exp(-g))
                go = jnp.concatenate([grads[q, own_cols] for q in token_rows], axis=0).astype(f32) * s
                dg = go * u * (1.0 + g * (1.0 - s))
                du = go * g
                scaled[unit, rows, 0:128] = (dg * fac_g).astype(bf16)
                scaled[unit, rows, 128:256] = (du * fac_u).astype(bf16)
                both = jnp.concatenate([dg * pre_g, du * pre_u], axis=1)
                return sums + jnp.sum(both.reshape(8, 8, 256), axis=0)

            sums = lax.fori_loop(0, 4, chunk, jnp.zeros((8, 256), f32))
            rc(scaled.at[unit], scaled.at[unit], c_s.at[unit], c_r.at[unit], end_of_mid).start()
            mags[pl.ds(unit, 1), :] = jnp.sum(sums, axis=0, keepdims=True) / norm

        return carry

    lax.fori_loop(0, GRAD + 2 * NB, step, 0)

    @pl.when(is_mid)
    def _():
        rc(mags, mags_in, mg_s.at[0], mg_r.at[0], end_of_mid).start()

    @pl.when(is_end)
    def _():
        lax.fori_loop(0, 2 * NB - 3, wait_scaled, 0)
        wait_scaled(2 * NB - 2, 0)

    def x_sum(buf):
        return buf[0].astype(f32) + buf[1].astype(f32) + buf[2].astype(f32) + buf[3].astype(f32)

    def gather(buf, me, peer, send, recv):
        def start():
            for d in (1, 2, 3):
                rc(buf.at[me], buf.at[me], send.at[d], recv.at[me], peer(d)).start()

        def wait():
            for d in (1, 2, 3):
                src = (me + d) % 4
                rc(buf.at[src], buf.at[src], send.at[d], recv.at[src], peer(d)).wait_recv()

        return start, wait

    bx_start, bx_wait = gather(br_x, x, xpeer, bx_s, bx_r)
    by_start, by_wait = gather(br_y, y, ypeer, by_s, by_r)
    bz_start, bz_wait = gather(br_z, z, zpeer, bz_s, bz_r)
    ux_start, ux_wait = gather(u_x, x, xpeer, ux_s, ux_r)

    def ga(h, d):
        target = (x + d) % 4
        return rc(ga_send.at[h, target], ga_recv.at[h, x], ga_s.at[h, d], ga_r.at[h, x], xpeer(d))

    def gb(h, d):
        target = (y + d) % 4
        return rc(gb_send.at[h, target], gb_recv.at[h, y], gb_s.at[h, d], gb_r.at[h, y], ypeer(d))

    def ga2(h, d):
        target = (y + d) % 4
        return rc(ga2_send.at[h, target], ga2_recv.at[h, y], ga2_s.at[h, d], ga2_r.at[h, y], ypeer(d))

    def gb2(h, d):
        target = (x + d) % 4
        return rc(gb2_send.at[h, target], gb2_recv.at[h, x], gb2_s.at[h, d], gb2_r.at[h, x], xpeer(d))

    def gz(h):
        return rc(gz_send.at[h], gz_recv.at[h], gz_s.at[h], gz_r.at[h], zhpeer)

    def first(h, block_of):
        def back_block(n, carry):
            rel = (1 + n) % 4
            target = (x + rel) % 4
            out = block_of(rel).astype(bf16).reshape(4, 2, 32, 512)
            ga_send[h, target] = out[:, 0]
            gb_send[h, :, target] = out[:, 1]

            @pl.when(n < 3)
            def _():
                ga(h, rel).start()

            return carry

        lax.fori_loop(0, 4, back_block, 0)
        for d in (1, 2, 3):
            gb(h, d).start()

    def received(send, recv, h, me):
        acc = send[h, me].astype(f32)
        for d in (1, 2, 3):
            acc = acc + recv[h, (me + d) % 4].astype(f32)
        return acc

    def wait_from(h, me, s_sem, r_sem, send, recv, peer):
        for d in (1, 2, 3):
            src = (me + d) % 4
            rc(send.at[h, src], recv.at[h, src], s_sem.at[h, d], r_sem.at[h, src], peer(d)).wait_recv()

    def second(h):
        wait_from(h, x, ga_s, ga_r, ga_send, ga_recv, xpeer)
        ga2_send[h] = received(ga_send, ga_recv, h, x).astype(bf16)
        for d in (1, 2, 3):
            ga2(h, d).start()
        wait_from(h, y, gb_s, gb_r, gb_send, gb_recv, ypeer)
        gb2_send[h] = received(gb_send, gb_recv, h, y).astype(bf16)
        for d in (1, 2, 3):
            gb2(h, d).start()

    def third(h):
        wait_from(h, y, ga2_s, ga2_r, ga2_send, ga2_recv, ypeer)
        acc_a = received(ga2_send, ga2_recv, h, y)
        wait_from(h, x, gb2_s, gb2_r, gb2_send, gb2_recv, xpeer)
        acc_b = received(gb2_send, gb2_recv, h, x)
        gz_send[h] = jnp.where(zh == 0, acc_b, acc_a).astype(bf16)
        gz(h).start()
        gz_keep[h] = jnp.where(zh == 0, acc_a, acc_b)

    def last(h):
        gz(h).wait_recv()
        return (gz_keep[h] + gz_recv[h].astype(f32)).astype(bf16)

    first(0, lambda rel: token_terms(0, rel, range(NB)))

    for d in (1, 2, 3):
        src = (y + d) % 4
        rc(in_y.at[src], in_y.at[src], iy_s.at[d], iy_r.at[src], ypeer(d)).wait_recv()
    in_all = in_y[...].reshape(4, 2, 2, 32, LANES)
    for h in range(2):
        inner[h] = in_all[:, :, h].reshape(256, LANES)

    def early(n, carry):
        token_sum[n] = token_terms(1, n, range(NB - 2))
        return carry

    lax.fori_loop(0, 4, early, 0)
    rank_sum[0] = rank_terms(0, range(NB))
    rank_sum[1] = rank_terms(1, range(NB - 2))
    for j in range(NB - 2):
        up_term(j)

    for d in (1, 2, 3):
        for h in range(2):
            token_x(h, d).wait_send()
            token_y(h, d, y).wait_send()
        rc(in_x.at[x], in_x.at[x], ix_s.at[d], ix_r.at[x], xpeer(d)).wait_send()
        rc(in_z.at[z], in_z.at[z], iz_s.at[d], iz_r.at[z], zpeer(d)).wait_send()
        rc(in_y.at[y], in_y.at[y], iy_s.at[d], iy_r.at[y], ypeer(d)).wait_send()
    def drain(j, carry):
        for d in (1, 2, 3):
            weights_x(j, d).wait_send()
        rc(w.at[j, dp], w.at[j, dp], f_s.at[j], f_r.at[j], sibling).wait_send()

        @pl.when(is_end)
        def _():
            rc(ss_own.at[j], ss_e.at[j], se_s.at[j], se_r.at[j], mid_of_end).wait_send()

        @pl.when(is_mid)
        def _():
            rc(ss_m_send.at[j], ss_m_recv.at[j], sm_s.at[j], sm_r.at[j], other_mid).wait_send()

        return carry

    def drain_unit(unit, carry):
        @pl.when(is_end)
        def _():
            rc(pe_send.at[unit], pe_recv.at[unit], e_s.at[unit], e_r.at[unit], mid_of_end).wait_send()

        @pl.when(is_mid)
        def _():
            rc(pm_send.at[unit], pm_recv.at[unit], m_s.at[unit], m_r.at[unit], other_mid).wait_send()
            rc(scaled.at[unit], scaled.at[unit], c_s.at[unit], c_r.at[unit], end_of_mid).wait_send()

        return carry

    lax.fori_loop(0, 2 * NB, drain_unit, 0)
    lax.fori_loop(0, NB, drain, 0)

    @pl.when(is_mid)
    def _():
        rc(mags, mags_in, mg_s.at[0], mg_r.at[0], end_of_mid).wait_send()

    @pl.when(is_end)
    def _():
        wait_scaled(2 * NB - 3, 0)
        wait_scaled(2 * NB - 1, 0)

    br_x[x, 0:64] = rank_sum[0].astype(bf16)
    br_x[x, 64:128] = (rank_sum[1] + rank_terms(1, range(NB - 2, NB))).astype(bf16)
    bx_start()

    first(1, lambda rel: token_sum[rel] + token_terms(1, rel, range(NB - 2, NB)))

    for j in range(NB - 2, NB):
        up_term(j)

    @pl.when(is_end)
    def _():
        rc(mags, mags_in, mg_s.at[0], mg_r.at[0], mid_of_end).wait_recv()
        mags[...] = mags_in[...]

    for j in range(NB):
        for p in range(2):
            u_part[p, 64:72, j * LANES : (j + 1) * LANES] = jnp.broadcast_to(
                mags[2 * j : 2 * j + 1, p * 128 : (p + 1) * 128]
                + mags[2 * j + 1 : 2 * j + 2, p * 128 : (p + 1) * 128],
                (8, LANES),
            )
    rc(u_part.at[1 - dp], u_recv, ud_s.at[0], ud_r.at[0], sibling).start()

    second(0)
    bx_wait()
    br_y[y] = x_sum(br_x).astype(bf16)
    by_start()
    rc(u_part.at[1 - dp], u_recv, ud_s.at[0], ud_r.at[0], sibling).wait_recv()
    u_x[x, 0:72] = (u_part[dp] + u_recv[...]).astype(bf16)
    u_x[x, 72:80] = jnp.zeros((8, NB * LANES), bf16)
    by_wait()
    br_zh_send[...] = x_sum(br_y).astype(bf16)
    rc(br_zh_send, br_zh_recv, bh_s.at[0], bh_r.at[0], zhpeer).start()
    third(0)
    second(1)
    ux_start()
    rc(br_zh_send, br_zh_recv, bh_s.at[0], bh_r.at[0], zhpeer).wait_recv()
    br_z[z] = (br_zh_send[...].astype(f32) + br_zh_recv[...].astype(f32)).astype(bf16)
    bz_start()
    third(1)
    bz_wait()
    ranks = br_z[...].reshape(4, 2, 2, 32, LANES)
    for h in range(2):
        br_all[:, :, h] = ranks[:, h]
    dg_send[...] = adapter_scale * dot_tn(tokens_ref[...], br_all[...].reshape(512, LANES))
    rc(dg_send, dg_recv, dg_s.at[0], dg_r.at[0], sibling).start()

    ux_wait()
    rc(u_x, u_other, uo_s.at[0], uo_r.at[0], sibling).start()
    u_ref[dp] = u_x[...]
    for h in range(2):
        final = last(h)
        tg_ref[h * 32 : (h + 1) * 32, :] = dot(final, perm[...]).astype(bf16)
    rc(dg_send, dg_recv, dg_s.at[0], dg_r.at[0], sibling).wait_recv()
    dg_ref[...] = dg_send[...] + dg_recv[...]
    rc(u_x, u_other, uo_s.at[0], uo_r.at[0], sibling).wait_recv()
    u_ref[1 - dp] = u_other[...]

    for d in (1, 2, 3):
        rc(br_x.at[x], br_x.at[x], bx_s.at[d], bx_r.at[x], xpeer(d)).wait_send()
        rc(br_y.at[y], br_y.at[y], by_s.at[d], by_r.at[y], ypeer(d)).wait_send()
        rc(br_z.at[z], br_z.at[z], bz_s.at[d], bz_r.at[z], zpeer(d)).wait_send()
        rc(u_x.at[x], u_x.at[x], ux_s.at[d], ux_r.at[x], xpeer(d)).wait_send()
        for h in range(2):
            ga(h, d).wait_send()
            gb(h, d).wait_send()
            ga2(h, d).wait_send()
            gb2(h, d).wait_send()
    rc(br_zh_send, br_zh_recv, bh_s.at[0], bh_r.at[0], zhpeer).wait_send()
    for h in range(2):
        gz(h).wait_send()
    rc(u_part.at[1 - dp], u_recv, ud_s.at[0], ud_r.at[0], sibling).wait_send()
    rc(u_x, u_other, uo_s.at[0], uo_r.at[0], sibling).wait_send()
    rc(dg_send, dg_recv, dg_s.at[0], dg_r.at[0], sibling).wait_send()


def finish(tg_in, dg_in, u_in, tg_ref, dg_ref, ug_ref, mg_ref):
    tg_ref[...] = tg_in[...]
    dg_ref[...] = dg_in[...]
    for p in range(2):
        for s in range(4):
            lanes = slice(s * NB * LANES, (s + 1) * NB * LANES)
            ug_ref[p, :, lanes] = u_in[p, s, 0:64].astype(f32)
            mg_ref[p : p + 1, lanes] = u_in[p, s, 64:80].astype(f32)[0:1]


def shards(tokens, levels, scales, down, up, magnitude, grad):
    V = pltpu.VMEM
    D = pltpu.SemaphoreType.DMA
    NU = 2 * NB
    buffers = [
        V((256, 3584), jnp.int32), V((512, 896), bf16), V((4, 2, 4, 64, 512), bf16), V((512, 512), bf16),
        V((512, 128), bf16), V((512, 128), bf16), V((NB, 2, 4, 512, 128), bf16), V((NB, 3, 512, 128), bf16),
        V((NU, 256, 256), f32), V((NU, 256, 256), bf16), V((NU, 256, 256), bf16),
        V((NU, 256, 256), bf16), V((NU, 256, 256), bf16),
        V((NB, 8, 256), f32), V((NB, 8, 256), f32), V((NB, 8, 256), f32), V((NB, 8, 256), f32),
        V((NU, 256, 256), bf16), V((16, 256), f32), V((16, 256), f32),
        V((4, 128, 128), bf16), V((4, 128, 128), bf16), V((4, 128, 128), bf16), V((NB, 128, 256), bf16),
        V((2, 4, 4, 32, 512), bf16), V((2, 4, 4, 32, 512), bf16), V((2, 4, 4, 32, 512), bf16), V((2, 4, 4, 32, 512), bf16),
        V((2, 4, 32, 512), bf16), V((2, 4, 32, 512), bf16), V((2, 4, 32, 512), bf16), V((2, 4, 32, 512), bf16),
        V((2, 32, 512), f32), V((2, 32, 512), bf16), V((2, 32, 512), bf16),
        V((4, 128, 128), bf16), V((4, 128, 128), bf16), V((128, 128), bf16), V((128, 128), bf16),
        V((4, 128, 128), bf16), V((512, 128), f32), V((512, 128), f32),
        V((2, 72, 896), f32), V((72, 896), f32), V((4, 80, 896), bf16), V((4, 80, 896), bf16),
        V((2, 256, 128), bf16), V((4, 256, 512), f32), V((2, 64, 128), f32), V((4, 2, 2, 32, 128), bf16),
    ]
    sems = [D((2,)), D((2, 4)), D((2, 4)), D((2, 4)), D((2, 4)), D((NB, 4)), D((NB, 4))]
    sems += [D((NB,)), D((NB,)), D((NU,)), D((NU,)), D((NB,)), D((NB,))]
    sems += [D((NU,)), D((NU,)), D((NB,)), D((NB,)), D((NU,)), D((NU,)), D((1,)), D((1,))]
    sems += [D((4,))] * 6
    sems += [D((2, 4))] * 8 + [D((2,))] * 2
    sems += [D((4,)), D((4,)), D((4,)), D((4,)), D((1,)), D((1,)), D((4,)), D((4,)), D((1,)), D((1,))]
    sems += [D((1,)), D((1,)), D((4,)), D((4,)), D((1,)), D((1,))]
    vm = pl.BlockSpec(memory_space=pltpu.VMEM)
    hbm = pl.BlockSpec(memory_space=pl.ANY)
    token_out, down_out, up_out = pl.pallas_call(
        kernel,
        out_shape=(
            jax.ShapeDtypeStruct((64, 512), bf16),
            jax.ShapeDtypeStruct((512, 128), f32),
            jax.ShapeDtypeStruct((2, 4, 80, 896), bf16),
        ),
        in_specs=[vm, hbm, vm, vm, vm, vm, hbm],
        out_specs=(vm, vm, vm),
        scratch_shapes=buffers + sems,
        compiler_params=pltpu.CompilerParams(
            collective_id=0, has_side_effects=True, vmem_limit_bytes=56 * 1024 * 1024
        ),
        name="qdora_backward",
    )(tokens, levels, scales, down, up.reshape(128, 3584), magnitude, grad)
    return pl.pallas_call(
        finish,
        out_shape=(
            jax.ShapeDtypeStruct((64, 512), bf16),
            jax.ShapeDtypeStruct((512, 128), f32),
            jax.ShapeDtypeStruct((2, 64, 3584), f32),
            jax.ShapeDtypeStruct((2, 3584), f32),
        ),
        in_specs=[vm] * 3,
        out_specs=(vm,) * 4,
        name="write_outputs",
    )(token_out, down_out, up_out)


def solution(mesh):
    placed = (
        P("dp", "row"),
        P(None, "row", "col"),
        P(None, "row", "col"),
        P("row", None),
        P(None, None, "col"),
        P(None, "col"),
        P("dp", "col"),
    )
    return jax.shard_map(
        shards,
        mesh=mesh,
        in_specs=placed,
        out_specs=(P(("dp", "col"), "row"), P("row", None), P(None, None, "col"), P(None, "col")),
        check_vma=False,
    )
```

```python
import functools

import jax
import jax.numpy as jnp
from jax import lax
from jax.experimental import pallas as pl
from jax.experimental.pallas import tpu as pltpu
from jax.sharding import PartitionSpec as P

normal_levels = (
    -1.0,
    -0.6961928009986877,
    -0.5250730514526367,
    -0.39491748809814453,
    -0.28444138169288635,
    -0.18477343022823334,
    -0.09105003625154495,
    0.0,
    0.07958029955625534,
    0.16093020141124725,
    0.24611230194568634,
    0.33791524171829224,
    0.44070982933044434,
    0.5626170039176941,
    0.7229568362236023,
    1.0,
)
adapter_scale = 2.0
norm_eps = 1e-06
MESH = pl.DeviceIdType.MESH
NB = 7
LANES = 128
LEAD = 4
PRE = LEAD + 2
MIX = PRE + 1
GRAD = MIX + 1
f32, bf16 = jnp.float32, jnp.bfloat16


def dot(a, b):
    return jnp.dot(a, b, preferred_element_type=f32)


def dot_nt(a, b):
    return lax.dot_general(a, b, (((1,), (1,)), ((), ())), preferred_element_type=f32)


def dot_tn(a, b):
    return lax.dot_general(a, b, (((0,), (0,)), ((), ())), preferred_element_type=f32)


def nibble_levels(words, shift):
    values = list(normal_levels)
    for bit in range(4):
        mask = jnp.bitwise_and(words, 1 << (shift + bit)) != 0
        values = [
            jnp.where(mask, values[2 * n + 1], values[2 * n]) for n in range(len(values) // 2)
        ]
    return values[0]


def kernel(
    tokens_ref, levels_hbm, scale_ref, down_ref, up_ref, mag_in_ref, grad_hbm,
    tg_ref, dg_ref, u_ref,
    levels, grads, tok, perm, a_perm, a_own, w, sbuf, own_part, pe_send, pe_recv, pm_send, pm_recv,
    ss_own, ss_e, ss_m_send, ss_m_recv, scaled, mags, mags_in,
    in_x, in_z, in_y, upb,
    ga_send, ga_recv, gb_send, gb_recv, ga2_send, ga2_recv, gb2_send, gb2_recv, gz_keep, gz_send, gz_recv,
    br_x, br_y, br_zh_send, br_zh_recv, br_z, dg_send, dg_recv,
    u_part, u_recv, u_x, u_other, inner, token_sum, rank_sum, br_all,
    local_sem, t_s, t_r, ty_s, ty_r, w_s, w_r, f_s, f_r, e_s, e_r, se_s, se_r, m_s, m_r, sm_s, sm_r, c_s, c_r, mg_s, mg_r,
    ix_s, ix_r, iz_s, iz_r, iy_s, iy_r,
    ga_s, ga_r, gb_s, gb_r, ga2_s, ga2_r, gb2_s, gb2_r, gz_s, gz_r,
    bx_s, bx_r, by_s, by_r, bh_s, bh_r, bz_s, bz_r, dg_s, dg_r,
    ud_s, ud_r, ux_s, ux_r, uo_s, uo_r,
):
    dp, row, col = lax.axis_index("dp"), lax.axis_index("row"), lax.axis_index("col")
    z, x = row // 4, row % 4
    y, zh = col // 2, col % 2

    def xpeer(d):
        return {"row": z * 4 + (x + d) % 4}

    def zpeer(d):
        return {"row": ((z + d) % 4) * 4 + x}

    def ypeer(d):
        return {"col": ((y + d) % 4) * 2 + zh}

    zhpeer = {"col": y * 2 + 1 - zh}
    sibling = {"dp": 1 - dp}
    is_mid = (z == 1) | (z == 2)
    is_end = (z == 0) | (z == 3)
    mid_of_end = {"row": jnp.where(z == 0, 1, 2) * 4 + x}
    end_of_mid = {"row": jnp.where(z == 1, 0, 3) * 4 + x}
    other_mid = {"row": jnp.where(z == 1, 2, 1) * 4 + x}

    def rc(src, dst, s, r, dev):
        return pltpu.make_async_remote_copy(
            src_ref=src, dst_ref=dst, send_sem=s, recv_sem=r, device_id=dev, device_id_type=MESH
        )

    lev_copy = pltpu.make_async_copy(levels_hbm.at[dp], levels, local_sem.at[0])
    lev_copy.start()
    grad_copy = pltpu.make_async_copy(
        grad_hbm.at[:, pl.ds(pl.multiple_of(x * (NB * LANES), LANES), NB * LANES)],
        grads, local_sem.at[1],
    )
    grad_copy.start()

    barrier = pltpu.get_barrier_semaphore()
    peers = [xpeer(d) for d in (1, 2, 3)] + [zpeer(d) for d in (1, 2, 3)]
    peers += [ypeer(d) for d in (1, 2, 3)] + [zhpeer, sibling]
    for dev in peers:
        pl.semaphore_signal(barrier, inc=1, device_id=dev, device_id_type=MESH)

    r_id = lax.broadcasted_iota(jnp.int32, (512, 512), 0)
    i_id = lax.broadcasted_iota(jnp.int32, (512, 512), 1)
    at = jnp.where(r_id < 256, 2 * r_id, 2 * r_id - 511)
    perm[...] = jnp.where(i_id == at, 1.0, 0.0).astype(bf16)
    own = dot_nt(tokens_ref[...], perm[...]).astype(bf16).reshape(4, 2, 2, 32, 512)
    for h in range(2):
        tok[0, h] = own[:, :, h].reshape(4, 64, 512)
    a_full = dot(perm[...], down_ref[...])
    a_perm[...] = a_full.astype(bf16)
    rank_id = lax.broadcasted_iota(jnp.int32, (512, LANES), 1)
    a_own[...] = jnp.where((rank_id >= 64) == (dp == 1), adapter_scale * a_full, 0.0).astype(bf16)
    pl.semaphore_wait(barrier, len(peers))

    def token_x(h, d):
        return rc(tok.at[0, h, y], tok.at[4 - d, h, y], t_s.at[h, d], t_r.at[h, 4 - d], xpeer(d))

    def token_y(h, d, q):
        part = tok.at[pl.ds(1, 3), h, q]
        return rc(part, part, ty_s.at[h, d], ty_r.at[h, q], ypeer(d))

    for d in (1, 2, 3):
        token_x(0, d).start()

    tok_y = tokens_ref[pl.ds(pl.multiple_of(y * 128, 128), 128), :]
    in_x[x] = dot(tok_y, down_ref[...]).astype(bf16)
    for d in (1, 2, 3):
        rc(in_x.at[x], in_x.at[x], ix_s.at[d], ix_r.at[x], xpeer(d)).start()

    for j in range(NB):
        cols = pl.ds(pl.multiple_of(x * (NB * LANES) + j * LANES, LANES), LANES)
        zero = jnp.zeros((64, LANES), bf16)
        upb[j, 0:64, 0:128] = up_ref[0:64, cols]
        upb[j, 64:128, 128:256] = up_ref[64:128, cols]
        upb[j, 0:64, 128:256] = zero
        upb[j, 64:128, 0:128] = zero
    mags[...] = jnp.zeros_like(mags)
    lev_copy.wait()

    def decode(j, target, store):
        cols = pl.ds(pl.multiple_of((target * NB + j) * LANES, LANES), LANES)
        words = levels[:, cols]
        scales = scale_ref[dp, :, cols]
        for k in range(2):
            lv = nibble_levels(words, 4 * k).reshape(8, 32, LANES)
            base = (lv * scales[:, None, :]).reshape(256, LANES)
            low = dot(a_own[k * 256 : (k + 1) * 256, :], up_ref[:, cols])
            store(k, (base + low).astype(bf16))

    def weights_x(j, d):
        return rc(sbuf.at[j, d - 1], w.at[j, dp, 4 - d], w_s.at[j, d], w_r.at[j, 4 - d], xpeer(d))

    def forward(j, rel):
        return rc(w.at[j, dp, rel], w.at[j, dp, rel], f_s.at[j, rel], f_r.at[j, rel], sibling)

    def place(turn):
        odd = turn % 2 == 1
        j = jnp.where(odd, (turn + 1) // 2, (turn - 2) // 2)
        h = jnp.where(odd, 0, 1)
        j = jnp.where(turn < 5, turn - 3, jnp.where(turn == 2 * NB - 1, NB - 1, j))
        h = jnp.where((turn < 5) | (turn == 2 * NB - 1), 1, h)
        j = jnp.where(turn < 3, turn, j)
        h = jnp.where(turn < 3, 0, h)
        return j, h, 2 * j + h

    z_rows = pl.ds(pl.multiple_of(z * 64, 64), 64)

    def token_terms(h, rel, blocks):
        acc = None
        for j in blocks:
            both = jnp.concatenate([w[j, 0, rel], w[j, 1, rel]], axis=1)
            term = dot_nt(scaled[2 * j + h], both)
            acc = term if acc is None else acc + term
        return acc

    def rank_terms(h, blocks):
        acc = None
        for j in blocks:
            term = dot_nt(scaled[2 * j + h, z_rows, :], upb[j])
            acc = term if acc is None else acc + term
        return acc

    def up_term(j):
        own_cols = slice(j * LANES, (j + 1) * LANES)
        full = dot_tn(inner[0], scaled[2 * j]) + dot_tn(inner[1], scaled[2 * j + 1])
        u_part[0, 0:64, own_cols] = adapter_scale * full[0:64, 0:128]
        u_part[1, 0:64, own_cols] = adapter_scale * full[64:128, 128:256]

    def piece(src, dst, s, r, unit, q, dev):
        rows = pl.ds(q * 128, 128)
        return rc(src.at[unit, rows], dst.at[unit, rows], s.at[unit, q], r.at[unit, q], dev)

    def to_mid(unit, q, dev):
        return piece(pe_send, pe_recv, e_s, e_r, unit, q, dev)

    def to_other(unit, q):
        return piece(pm_send, pm_recv, m_s, m_r, unit, q, other_mid)

    def to_end(unit, q, dev):
        return piece(scaled, scaled, c_s, c_r, unit, q, dev)

    def wait_scaled(unit, carry):
        for q in range(2):
            to_end(unit, q, mid_of_end).wait_recv()
        return carry

    def step(it, carry):
        @pl.when((it % 2 == 0) & (it < 2 * NB))
        def _():
            j = it // 2
            for d in (1, 2, 3):
                def put(k, v, d=d):
                    sbuf[j, d - 1, k * 256 : (k + 1) * 256, :] = v

                decode(j, (x + d) % 4, put)
                weights_x(j, d).start()

            def put_own(k, v):
                w[j, dp, 0, k * 256 : (k + 1) * 256, :] = v

            decode(j, x, put_own)
            forward(j, 0).start()

        @pl.when(it == 1)
        def _():
            for d in (1, 2, 3):
                token_x(1, d).start()
            for d in (1, 2, 3):
                token_x(0, d).wait_recv()
            for d in (1, 2, 3):
                token_y(0, d, y).start()

        @pl.when(it == 7)
        def _():
            for d in (1, 2, 3):
                src = (x + d) % 4
                rc(in_x.at[src], in_x.at[src], ix_s.at[d], ix_r.at[src], xpeer(d)).wait_recv()
            total = in_x[0].astype(f32) + in_x[1].astype(f32) + in_x[2].astype(f32) + in_x[3].astype(f32)
            in_z[z] = total.astype(bf16)
            for d in (1, 2, 3):
                rc(in_z.at[z], in_z.at[z], iz_s.at[d], iz_r.at[z], zpeer(d)).start()

        @pl.when(it == 11)
        def _():
            for d in (1, 2, 3):
                src = (z + d) % 4
                rc(in_z.at[src], in_z.at[src], iz_s.at[d], iz_r.at[src], zpeer(d)).wait_recv()
            total = in_z[0].astype(f32) + in_z[1].astype(f32) + in_z[2].astype(f32) + in_z[3].astype(f32)
            in_y[y] = total.astype(bf16)
            for d in (1, 2, 3):
                rc(in_y.at[y], in_y.at[y], iy_s.at[d], iy_r.at[y], ypeer(d)).start()

        @pl.when(it == PRE)
        def _():
            for d in (1, 2, 3):
                token_x(1, d).wait_recv()
            for d in (1, 2, 3):
                token_y(0, d, (y + d) % 4).wait_recv()
            for d in (1, 2, 3):
                token_y(1, d, y).start()

        @pl.when(it == PRE + 3)
        def _():
            for d in (1, 2, 3):
                token_y(1, d, (y + d) % 4).wait_recv()

        @pl.when((it >= PRE) & (it < PRE + 2 * NB))
        def _():
            j, h, unit = place(it - PRE)

            @pl.when(h == 0)
            def _():
                for rel in range(4):
                    rc(w.at[j, 1 - dp, rel], w.at[j, 1 - dp, rel], f_s.at[j, rel], f_r.at[j, rel], sibling).wait_recv()
                ss = None
                for s in range(4):
                    wide = jnp.concatenate([w[j, 0, s], w[j, 1, s]], axis=1).astype(f32)
                    sq = jnp.sum((wide * wide).reshape(64, 8, 256), axis=0)
                    ss = sq if ss is None else ss + sq
                ss_own[j] = ss

                @pl.when(is_end)
                def _():
                    rc(ss_own.at[j], ss_e.at[j], se_s.at[j], se_r.at[j], mid_of_end).start()

            part = None
            for s in range(4):
                both = jnp.concatenate([w[j, 0, s], w[j, 1, s]], axis=1)
                term = dot(tok[s, h].reshape(256, 512), both)
                part = term if part is None else part + term

            @pl.when(is_end)
            def _():
                pe_send[unit] = part.astype(bf16)
                for q in range(2):
                    to_mid(unit, q, mid_of_end).start()

            @pl.when(is_mid)
            def _():
                own_part[unit] = part

        early = (it >= PRE - 1) & (it < PRE + 2)
        late = (it % 2 == 0) & (it >= LEAD + 6) & (it < LEAD + 2 * NB)

        @pl.when(early | late)
        def _():
            j = jnp.where(early, it - (PRE - 1), (it - LEAD) // 2)
            for d in (1, 3, 2):
                weights_x(j, d).wait_recv()
                forward(j, 4 - d).start()

        @pl.when(is_mid & (it >= MIX) & (it < MIX + 2 * NB))
        def _():
            j, h, unit = place(it - MIX)

            @pl.when(h == 0)
            def _():
                rc(ss_own.at[j], ss_e.at[j], se_s.at[j], se_r.at[j], end_of_mid).wait_recv()
                ss_m_send[j] = ss_own[j] + ss_e[j]
                rc(ss_m_send.at[j], ss_m_recv.at[j], sm_s.at[j], sm_r.at[j], other_mid).start()

            for q in range(2):
                to_mid(unit, q, end_of_mid).wait_recv()
                rows = pl.ds(q * 128, 128)
                pm_send[unit, rows] = (own_part[unit, rows] + pe_recv[unit, rows].astype(f32)).astype(bf16)
                to_other(unit, q).start()

        @pl.when(it == GRAD)
        def _():
            grad_copy.wait()

        @pl.when(is_mid & (it >= GRAD) & (it < GRAD + 2 * NB))
        def _():
            j, h, unit = place(it - GRAD)

            @pl.when(h == 0)
            def _():
                rc(ss_m_send.at[j], ss_m_recv.at[j], sm_s.at[j], sm_r.at[j], other_mid).wait_recv()

            squares = jnp.sum(ss_m_send[j] + ss_m_recv[j], axis=0, keepdims=True)
            norm = jnp.sqrt(squares + norm_eps)
            cols = pl.ds(pl.multiple_of(x * (NB * LANES) + j * LANES, LANES), LANES)
            fac_g = mag_in_ref[0:1, cols] / norm[:, 0:128]
            fac_u = mag_in_ref[1:2, cols] / norm[:, 128:256]
            own_cols = pl.ds(pl.multiple_of(j * LANES, LANES), LANES)

            def chunk(n, sums):
                rows = pl.ds(pl.multiple_of(n * 64, 64), 64)
                token_rows = [pl.ds(pl.multiple_of(n * 128 + q * 64 + h * 32, 32), 32) for q in range(2)]
                pre = pm_send[unit, rows, :].astype(f32) + pm_recv[unit, rows, :].astype(f32)
                pre_g, pre_u = pre[:, 0:128], pre[:, 128:256]
                g, u = pre_g * fac_g, pre_u * fac_u
                s = 1.0 / (1.0 + jnp.exp(-g))
                go = jnp.concatenate([grads[q, own_cols] for q in token_rows], axis=0).astype(f32) * s
                dg = go * u * (1.0 + g * (1.0 - s))
                du = go * g
                scaled[unit, rows, 0:128] = (dg * fac_g).astype(bf16)
                scaled[unit, rows, 128:256] = (du * fac_u).astype(bf16)
                both = jnp.concatenate([dg * pre_g, du * pre_u], axis=1)
                return sums + jnp.sum(both.reshape(8, 8, 256), axis=0)

            sums = jnp.zeros((8, 256), f32)
            for q in range(2):
                to_other(unit, q).wait_recv()
                sums = lax.fori_loop(2 * q, 2 * q + 2, chunk, sums)
                to_end(unit, q, end_of_mid).start()
            mags[pl.ds(unit, 1), :] = jnp.sum(sums, axis=0, keepdims=True) / norm

        return carry

    lax.fori_loop(0, GRAD + 2 * NB, step, 0)

    @pl.when(is_mid)
    def _():
        rc(mags, mags_in, mg_s.at[0], mg_r.at[0], end_of_mid).start()

    @pl.when(is_end)
    def _():
        lax.fori_loop(0, 2 * NB - 3, wait_scaled, 0)
        wait_scaled(2 * NB - 2, 0)

    def x_sum(buf):
        return buf[0].astype(f32) + buf[1].astype(f32) + buf[2].astype(f32) + buf[3].astype(f32)

    def gather(buf, me, peer, send, recv):
        def start():
            for d in (1, 2, 3):
                rc(buf.at[me], buf.at[me], send.at[d], recv.at[me], peer(d)).start()

        def wait():
            for d in (1, 2, 3):
                src = (me + d) % 4
                rc(buf.at[src], buf.at[src], send.at[d], recv.at[src], peer(d)).wait_recv()

        return start, wait

    bx_start, bx_wait = gather(br_x, x, xpeer, bx_s, bx_r)
    by_start, by_wait = gather(br_y, y, ypeer, by_s, by_r)
    bz_start, bz_wait = gather(br_z, z, zpeer, bz_s, bz_r)
    ux_start, ux_wait = gather(u_x, x, xpeer, ux_s, ux_r)

    def ga(h, d):
        target = (x + d) % 4
        return rc(ga_send.at[h, target], ga_recv.at[h, x], ga_s.at[h, d], ga_r.at[h, x], xpeer(d))

    def gb(h, d):
        target = (y + d) % 4
        return rc(gb_send.at[h, target], gb_recv.at[h, y], gb_s.at[h, d], gb_r.at[h, y], ypeer(d))

    def ga2(h, d):
        target = (y + d) % 4
        return rc(ga2_send.at[h, target], ga2_recv.at[h, y], ga2_s.at[h, d], ga2_r.at[h, y], ypeer(d))

    def gb2(h, d):
        target = (x + d) % 4
        return rc(gb2_send.at[h, target], gb2_recv.at[h, x], gb2_s.at[h, d], gb2_r.at[h, x], xpeer(d))

    def gz(h):
        return rc(gz_send.at[h], gz_recv.at[h], gz_s.at[h], gz_r.at[h], zhpeer)

    def first(h, block_of):
        def back_block(n, carry):
            rel = (1 + n) % 4
            target = (x + rel) % 4
            out = block_of(rel).astype(bf16).reshape(4, 2, 32, 512)
            ga_send[h, target] = out[:, 0]
            gb_send[h, :, target] = out[:, 1]

            @pl.when(n < 3)
            def _():
                ga(h, rel).start()

            return carry

        lax.fori_loop(0, 4, back_block, 0)
        for d in (1, 2, 3):
            gb(h, d).start()

    def received(send, recv, h, me):
        acc = send[h, me].astype(f32)
        for d in (1, 2, 3):
            acc = acc + recv[h, (me + d) % 4].astype(f32)
        return acc

    def wait_from(h, me, s_sem, r_sem, send, recv, peer):
        for d in (1, 2, 3):
            src = (me + d) % 4
            rc(send.at[h, src], recv.at[h, src], s_sem.at[h, d], r_sem.at[h, src], peer(d)).wait_recv()

    def second(h):
        wait_from(h, x, ga_s, ga_r, ga_send, ga_recv, xpeer)
        ga2_send[h] = received(ga_send, ga_recv, h, x).astype(bf16)
        for d in (1, 2, 3):
            ga2(h, d).start()
        wait_from(h, y, gb_s, gb_r, gb_send, gb_recv, ypeer)
        gb2_send[h] = received(gb_send, gb_recv, h, y).astype(bf16)
        for d in (1, 2, 3):
            gb2(h, d).start()

    def third(h):
        wait_from(h, y, ga2_s, ga2_r, ga2_send, ga2_recv, ypeer)
        acc_a = received(ga2_send, ga2_recv, h, y)
        wait_from(h, x, gb2_s, gb2_r, gb2_send, gb2_recv, xpeer)
        acc_b = received(gb2_send, gb2_recv, h, x)
        gz_send[h] = jnp.where(zh == 0, acc_b, acc_a).astype(bf16)
        gz(h).start()
        gz_keep[h] = jnp.where(zh == 0, acc_a, acc_b)

    def last(h):
        gz(h).wait_recv()
        return (gz_keep[h] + gz_recv[h].astype(f32)).astype(bf16)

    first(0, lambda rel: token_terms(0, rel, range(NB)))

    for d in (1, 2, 3):
        src = (y + d) % 4
        rc(in_y.at[src], in_y.at[src], iy_s.at[d], iy_r.at[src], ypeer(d)).wait_recv()
    in_all = in_y[...].reshape(4, 2, 2, 32, LANES)
    for h in range(2):
        inner[h] = in_all[:, :, h].reshape(256, LANES)

    def early(n, carry):
        token_sum[n] = token_terms(1, n, range(NB - 2))
        return carry

    lax.fori_loop(0, 4, early, 0)
    rank_sum[0] = rank_terms(0, range(NB))
    rank_sum[1] = rank_terms(1, range(NB - 2))
    for j in range(NB - 2):
        up_term(j)

    @pl.when(is_end)
    def _():
        wait_scaled(2 * NB - 3, 0)
        wait_scaled(2 * NB - 1, 0)

    br_zh_send[0:64] = rank_sum[0].astype(bf16)
    br_zh_send[64:128] = (rank_sum[1] + rank_terms(1, range(NB - 2, NB))).astype(bf16)
    rc(br_zh_send, br_zh_recv, bh_s.at[0], bh_r.at[0], zhpeer).start()

    first(1, lambda rel: token_sum[rel] + token_terms(1, rel, range(NB - 2, NB)))

    for j in range(NB - 2, NB):
        up_term(j)

    @pl.when(is_end)
    def _():
        rc(mags, mags_in, mg_s.at[0], mg_r.at[0], mid_of_end).wait_recv()
        mags[...] = mags_in[...]

    for j in range(NB):
        for p in range(2):
            u_part[p, 64:72, j * LANES : (j + 1) * LANES] = jnp.broadcast_to(
                mags[2 * j : 2 * j + 1, p * 128 : (p + 1) * 128]
                + mags[2 * j + 1 : 2 * j + 2, p * 128 : (p + 1) * 128],
                (8, LANES),
            )
    rc(u_part.at[1 - dp], u_recv, ud_s.at[0], ud_r.at[0], sibling).start()

    for d in (1, 2, 3):
        for h in range(2):
            token_x(h, d).wait_send()
            token_y(h, d, y).wait_send()
        rc(in_x.at[x], in_x.at[x], ix_s.at[d], ix_r.at[x], xpeer(d)).wait_send()
        rc(in_z.at[z], in_z.at[z], iz_s.at[d], iz_r.at[z], zpeer(d)).wait_send()
        rc(in_y.at[y], in_y.at[y], iy_s.at[d], iy_r.at[y], ypeer(d)).wait_send()
    def drain(j, carry):
        for d in (1, 2, 3):
            weights_x(j, d).wait_send()
        for rel in range(4):
            forward(j, rel).wait_send()

        @pl.when(is_end)
        def _():
            rc(ss_own.at[j], ss_e.at[j], se_s.at[j], se_r.at[j], mid_of_end).wait_send()

        @pl.when(is_mid)
        def _():
            rc(ss_m_send.at[j], ss_m_recv.at[j], sm_s.at[j], sm_r.at[j], other_mid).wait_send()

        return carry

    def drain_unit(unit, carry):
        @pl.when(is_end)
        def _():
            for q in range(2):
                to_mid(unit, q, mid_of_end).wait_send()

        @pl.when(is_mid)
        def _():
            for q in range(2):
                to_other(unit, q).wait_send()
                to_end(unit, q, end_of_mid).wait_send()

        return carry

    lax.fori_loop(0, 2 * NB, drain_unit, 0)
    lax.fori_loop(0, NB, drain, 0)

    @pl.when(is_mid)
    def _():
        rc(mags, mags_in, mg_s.at[0], mg_r.at[0], end_of_mid).wait_send()

    second(0)
    rc(u_part.at[1 - dp], u_recv, ud_s.at[0], ud_r.at[0], sibling).wait_recv()
    u_x[x, 0:72] = (u_part[dp] + u_recv[...]).astype(bf16)
    u_x[x, 72:80] = jnp.zeros((8, NB * LANES), bf16)
    rc(br_zh_send, br_zh_recv, bh_s.at[0], bh_r.at[0], zhpeer).wait_recv()
    br_x[x] = (br_zh_send[...].astype(f32) + br_zh_recv[...].astype(f32)).astype(bf16)
    bx_start()
    third(0)
    bx_wait()
    br_y[y] = x_sum(br_x).astype(bf16)
    by_start()
    second(1)
    ux_start()
    by_wait()
    br_z[z] = x_sum(br_y).astype(bf16)
    bz_start()
    third(1)
    bz_wait()
    ranks = br_z[...].reshape(4, 2, 2, 32, LANES)
    for h in range(2):
        br_all[:, :, h] = ranks[:, h]
    dg_send[...] = adapter_scale * dot_tn(tokens_ref[...], br_all[...].reshape(512, LANES))
    rc(dg_send, dg_recv, dg_s.at[0], dg_r.at[0], sibling).start()

    ux_wait()
    rc(u_x, u_other, uo_s.at[0], uo_r.at[0], sibling).start()
    u_ref[dp] = u_x[...]
    for h in range(2):
        final = last(h)
        tg_ref[h * 32 : (h + 1) * 32, :] = dot(final, perm[...]).astype(bf16)
    rc(dg_send, dg_recv, dg_s.at[0], dg_r.at[0], sibling).wait_recv()
    dg_ref[...] = dg_send[...] + dg_recv[...]
    rc(u_x, u_other, uo_s.at[0], uo_r.at[0], sibling).wait_recv()
    u_ref[1 - dp] = u_other[...]

    for d in (1, 2, 3):
        rc(br_x.at[x], br_x.at[x], bx_s.at[d], bx_r.at[x], xpeer(d)).wait_send()
        rc(br_y.at[y], br_y.at[y], by_s.at[d], by_r.at[y], ypeer(d)).wait_send()
        rc(br_z.at[z], br_z.at[z], bz_s.at[d], bz_r.at[z], zpeer(d)).wait_send()
        rc(u_x.at[x], u_x.at[x], ux_s.at[d], ux_r.at[x], xpeer(d)).wait_send()
        for h in range(2):
            ga(h, d).wait_send()
            gb(h, d).wait_send()
            ga2(h, d).wait_send()
            gb2(h, d).wait_send()
    rc(br_zh_send, br_zh_recv, bh_s.at[0], bh_r.at[0], zhpeer).wait_send()
    for h in range(2):
        gz(h).wait_send()
    rc(u_part.at[1 - dp], u_recv, ud_s.at[0], ud_r.at[0], sibling).wait_send()
    rc(u_x, u_other, uo_s.at[0], uo_r.at[0], sibling).wait_send()
    rc(dg_send, dg_recv, dg_s.at[0], dg_r.at[0], sibling).wait_send()


def finish(tg_in, dg_in, u_in, tg_ref, dg_ref, ug_ref, mg_ref):
    tg_ref[...] = tg_in[...]
    dg_ref[...] = dg_in[...]
    for p in range(2):
        for s in range(4):
            lanes = slice(s * NB * LANES, (s + 1) * NB * LANES)
            ug_ref[p, :, lanes] = u_in[p, s, 0:64].astype(f32)
            mg_ref[p : p + 1, lanes] = u_in[p, s, 64:80].astype(f32)[0:1]


def shards(tokens, levels, scales, down, up, magnitude, grad):
    V = pltpu.VMEM
    D = pltpu.SemaphoreType.DMA
    NU = 2 * NB
    buffers = [
        V((256, 3584), jnp.int32), V((512, 896), bf16), V((4, 2, 4, 64, 512), bf16), V((512, 512), bf16),
        V((512, 128), bf16), V((512, 128), bf16), V((NB, 2, 4, 512, 128), bf16), V((NB, 3, 512, 128), bf16),
        V((NU, 256, 256), f32), V((NU, 256, 256), bf16), V((NU, 256, 256), bf16),
        V((NU, 256, 256), bf16), V((NU, 256, 256), bf16),
        V((NB, 8, 256), f32), V((NB, 8, 256), f32), V((NB, 8, 256), f32), V((NB, 8, 256), f32),
        V((NU, 256, 256), bf16), V((16, 256), f32), V((16, 256), f32),
        V((4, 128, 128), bf16), V((4, 128, 128), bf16), V((4, 128, 128), bf16), V((NB, 128, 256), bf16),
        V((2, 4, 4, 32, 512), bf16), V((2, 4, 4, 32, 512), bf16), V((2, 4, 4, 32, 512), bf16), V((2, 4, 4, 32, 512), bf16),
        V((2, 4, 32, 512), bf16), V((2, 4, 32, 512), bf16), V((2, 4, 32, 512), bf16), V((2, 4, 32, 512), bf16),
        V((2, 32, 512), f32), V((2, 32, 512), bf16), V((2, 32, 512), bf16),
        V((4, 128, 128), bf16), V((4, 128, 128), bf16), V((128, 128), bf16), V((128, 128), bf16),
        V((4, 128, 128), bf16), V((512, 128), f32), V((512, 128), f32),
        V((2, 72, 896), f32), V((72, 896), f32), V((4, 80, 896), bf16), V((4, 80, 896), bf16),
        V((2, 256, 128), bf16), V((4, 256, 512), f32), V((2, 64, 128), f32), V((4, 2, 2, 32, 128), bf16),
    ]
    sems = [D((2,)), D((2, 4)), D((2, 4)), D((2, 4)), D((2, 4)), D((NB, 4)), D((NB, 4))]
    sems += [D((NB, 4)), D((NB, 4)), D((NU, 2)), D((NU, 2)), D((NB,)), D((NB,))]
    sems += [D((NU, 2)), D((NU, 2)), D((NB,)), D((NB,)), D((NU, 2)), D((NU, 2)), D((1,)), D((1,))]
    sems += [D((4,))] * 6
    sems += [D((2, 4))] * 8 + [D((2,))] * 2
    sems += [D((4,)), D((4,)), D((4,)), D((4,)), D((1,)), D((1,)), D((4,)), D((4,)), D((1,)), D((1,))]
    sems += [D((1,)), D((1,)), D((4,)), D((4,)), D((1,)), D((1,))]
    vm = pl.BlockSpec(memory_space=pltpu.VMEM)
    hbm = pl.BlockSpec(memory_space=pl.ANY)
    token_out, down_out, up_out = pl.pallas_call(
        kernel,
        out_shape=(
            jax.ShapeDtypeStruct((64, 512), bf16),
            jax.ShapeDtypeStruct((512, 128), f32),
            jax.ShapeDtypeStruct((2, 4, 80, 896), bf16),
        ),
        in_specs=[vm, hbm, vm, vm, vm, vm, hbm],
        out_specs=(vm, vm, vm),
        scratch_shapes=buffers + sems,
        compiler_params=pltpu.CompilerParams(
            collective_id=0, has_side_effects=True, vmem_limit_bytes=56 * 1024 * 1024
        ),
        name="qdora_backward",
    )(tokens, levels, scales, down, up.reshape(128, 3584), magnitude, grad)
    return pl.pallas_call(
        finish,
        out_shape=(
            jax.ShapeDtypeStruct((64, 512), bf16),
            jax.ShapeDtypeStruct((512, 128), f32),
            jax.ShapeDtypeStruct((2, 64, 3584), f32),
            jax.ShapeDtypeStruct((2, 3584), f32),
        ),
        in_specs=[vm] * 3,
        out_specs=(vm,) * 4,
        name="write_outputs",
    )(token_out, down_out, up_out)


def solution(mesh):
    placed = (
        P("dp", "row"),
        P(None, "row", "col"),
        P(None, "row", "col"),
        P("row", None),
        P(None, None, "col"),
        P(None, "col"),
        P("dp", "col"),
    )
    return jax.shard_map(
        shards,
        mesh=mesh,
        in_specs=placed,
        out_specs=(P(("dp", "col"), "row"), P("row", None), P(None, None, "col"), P(None, "col")),
        check_vma=False,
    )
```

```python
import functools

import jax
import jax.numpy as jnp
from jax import lax
from jax.experimental import pallas as pl
from jax.experimental.pallas import tpu as pltpu
from jax.sharding import PartitionSpec as P

normal_levels = (
    -1.0,
    -0.6961928009986877,
    -0.5250730514526367,
    -0.39491748809814453,
    -0.28444138169288635,
    -0.18477343022823334,
    -0.09105003625154495,
    0.0,
    0.07958029955625534,
    0.16093020141124725,
    0.24611230194568634,
    0.33791524171829224,
    0.44070982933044434,
    0.5626170039176941,
    0.7229568362236023,
    1.0,
)
adapter_scale = 2.0
norm_eps = 1e-06
MESH = pl.DeviceIdType.MESH
NB = 7
LANES = 128
LEAD = 4
PRE = LEAD + 2
MIX = PRE + 1
GRAD = MIX + 1
f32, bf16 = jnp.float32, jnp.bfloat16


def dot(a, b):
    return jnp.dot(a, b, preferred_element_type=f32)


def dot_nt(a, b):
    return lax.dot_general(a, b, (((1,), (1,)), ((), ())), preferred_element_type=f32)


def dot_tn(a, b):
    return lax.dot_general(a, b, (((0,), (0,)), ((), ())), preferred_element_type=f32)


def nibble_levels(words, shift):
    values = list(normal_levels)
    for bit in range(4):
        mask = jnp.bitwise_and(words, 1 << (shift + bit)) != 0
        values = [
            jnp.where(mask, values[2 * n + 1], values[2 * n]) for n in range(len(values) // 2)
        ]
    return values[0]


def kernel(
    tokens_ref, levels_hbm, scale_ref, down_ref, up_ref, mag_in_ref, grad_hbm,
    tg_ref, dg_ref, u_ref,
    levels, grads, tok, perm, a_perm, a_own, w, sbuf, own_part, pe_send, pe_recv, pm_send, pm_recv,
    ss_own, ss_e, ss_m_send, ss_m_recv, scaled, mags, mags_in,
    in_x, in_z, in_y, upb,
    ga_send, ga_recv, gb_send, gb_recv, ga2_send, ga2_recv, gb2_send, gb2_recv, gz_keep, gz_send, gz_recv,
    br_x, br_y, br_zh_send, br_zh_recv, br_z, dg_send, dg_recv,
    u_part, u_recv, u_x, u_other, inner, token_sum, rank_sum, br_all,
    local_sem, t_s, t_r, ty_s, ty_r, w_s, w_r, f_s, f_r, e_s, e_r, se_s, se_r, m_s, m_r, sm_s, sm_r, c_s, c_r, mg_s, mg_r,
    ix_s, ix_r, iz_s, iz_r, iy_s, iy_r,
    ga_s, ga_r, gb_s, gb_r, ga2_s, ga2_r, gb2_s, gb2_r, gz_s, gz_r,
    bx_s, bx_r, by_s, by_r, bh_s, bh_r, bz_s, bz_r, dg_s, dg_r,
    ud_s, ud_r, ux_s, ux_r, uo_s, uo_r,
):
    dp, row, col = lax.axis_index("dp"), lax.axis_index("row"), lax.axis_index("col")
    z, x = row // 4, row % 4
    y, zh = col // 2, col % 2

    def xpeer(d):
        return {"row": z * 4 + (x + d) % 4}

    def zpeer(d):
        return {"row": ((z + d) % 4) * 4 + x}

    def ypeer(d):
        return {"col": ((y + d) % 4) * 2 + zh}

    zhpeer = {"col": y * 2 + 1 - zh}
    sibling = {"dp": 1 - dp}
    is_mid = (z == 1) | (z == 2)
    is_end = (z == 0) | (z == 3)
    mid_of_end = {"row": jnp.where(z == 0, 1, 2) * 4 + x}
    end_of_mid = {"row": jnp.where(z == 1, 0, 3) * 4 + x}
    other_mid = {"row": jnp.where(z == 1, 2, 1) * 4 + x}

    def rc(src, dst, s, r, dev):
        return pltpu.make_async_remote_copy(
            src_ref=src, dst_ref=dst, send_sem=s, recv_sem=r, device_id=dev, device_id_type=MESH
        )

    lev_copy = pltpu.make_async_copy(levels_hbm.at[dp], levels, local_sem.at[0])
    lev_copy.start()
    grad_copy = pltpu.make_async_copy(
        grad_hbm.at[:, pl.ds(pl.multiple_of(x * (NB * LANES), LANES), NB * LANES)],
        grads, local_sem.at[1],
    )
    grad_copy.start()

    barrier = pltpu.get_barrier_semaphore()
    peers = [xpeer(d) for d in (1, 2, 3)] + [zpeer(d) for d in (1, 2, 3)]
    peers += [ypeer(d) for d in (1, 2, 3)] + [zhpeer, sibling]
    for dev in peers:
        pl.semaphore_signal(barrier, inc=1, device_id=dev, device_id_type=MESH)

    r_id = lax.broadcasted_iota(jnp.int32, (512, 512), 0)
    i_id = lax.broadcasted_iota(jnp.int32, (512, 512), 1)
    at = jnp.where(r_id < 256, 2 * r_id, 2 * r_id - 511)
    perm[...] = jnp.where(i_id == at, 1.0, 0.0).astype(bf16)
    own = dot_nt(tokens_ref[...], perm[...]).astype(bf16).reshape(4, 2, 2, 32, 512)
    for h in range(2):
        tok[0, h] = own[:, :, h].reshape(4, 64, 512)
    a_full = dot(perm[...], down_ref[...])
    a_perm[...] = a_full.astype(bf16)
    rank_id = lax.broadcasted_iota(jnp.int32, (512, LANES), 1)
    a_own[...] = jnp.where((rank_id >= 64) == (dp == 1), adapter_scale * a_full, 0.0).astype(bf16)
    pl.semaphore_wait(barrier, len(peers))

    def token_x(h, d):
        return rc(tok.at[0, h, y], tok.at[4 - d, h, y], t_s.at[h, d], t_r.at[h, 4 - d], xpeer(d))

    def token_y(h, d, q):
        part = tok.at[pl.ds(1, 3), h, q]
        return rc(part, part, ty_s.at[h, d], ty_r.at[h, q], ypeer(d))

    for d in (1, 2, 3):
        token_x(0, d).start()

    tok_y = tokens_ref[pl.ds(pl.multiple_of(y * 128, 128), 128), :]
    in_x[x] = dot(tok_y, down_ref[...]).astype(bf16)
    for d in (1, 2, 3):
        rc(in_x.at[x], in_x.at[x], ix_s.at[d], ix_r.at[x], xpeer(d)).start()

    for j in range(NB):
        cols = pl.ds(pl.multiple_of(x * (NB * LANES) + j * LANES, LANES), LANES)
        zero = jnp.zeros((64, LANES), bf16)
        upb[j, 0:64, 0:128] = up_ref[0:64, cols]
        upb[j, 64:128, 128:256] = up_ref[64:128, cols]
        upb[j, 0:64, 128:256] = zero
        upb[j, 64:128, 0:128] = zero
    mags[...] = jnp.zeros_like(mags)
    lev_copy.wait()

    def decode(j, target, store):
        cols = pl.ds(pl.multiple_of((target * NB + j) * LANES, LANES), LANES)
        words = levels[:, cols]
        scales = scale_ref[dp, :, cols]
        for k in range(2):
            lv = nibble_levels(words, 4 * k).reshape(8, 32, LANES)
            base = (lv * scales[:, None, :]).reshape(256, LANES)
            low = dot(a_own[k * 256 : (k + 1) * 256, :], up_ref[:, cols])
            store(k, (base + low).astype(bf16))

    def weights_x(j, d):
        return rc(sbuf.at[j, d - 1], w.at[j, dp, 4 - d], w_s.at[j, d], w_r.at[j, 4 - d], xpeer(d))

    def forward(j, rel):
        return rc(w.at[j, dp, rel], w.at[j, dp, rel], f_s.at[j, rel], f_r.at[j, rel], sibling)

    def place(turn):
        odd = turn % 2 == 1
        j = jnp.where(odd, (turn + 1) // 2, (turn - 2) // 2)
        h = jnp.where(odd, 0, 1)
        j = jnp.where(turn < 5, turn - 3, jnp.where(turn == 2 * NB - 1, NB - 1, j))
        h = jnp.where((turn < 5) | (turn == 2 * NB - 1), 1, h)
        j = jnp.where(turn < 3, turn, j)
        h = jnp.where(turn < 3, 0, h)
        return j, h, 2 * j + h

    z_rows = pl.ds(pl.multiple_of(z * 64, 64), 64)

    def token_terms(h, rel, blocks):
        acc = None
        for j in blocks:
            both = jnp.concatenate([w[j, 0, rel], w[j, 1, rel]], axis=1)
            term = dot_nt(scaled[2 * j + h], both)
            acc = term if acc is None else acc + term
        return acc

    def rank_terms(h, blocks):
        acc = None
        for j in blocks:
            term = dot_nt(scaled[2 * j + h, z_rows, :], upb[j])
            acc = term if acc is None else acc + term
        return acc

    def up_term(j):
        own_cols = slice(j * LANES, (j + 1) * LANES)
        full = dot_tn(inner[0], scaled[2 * j]) + dot_tn(inner[1], scaled[2 * j + 1])
        u_part[0, 0:64, own_cols] = adapter_scale * full[0:64, 0:128]
        u_part[1, 0:64, own_cols] = adapter_scale * full[64:128, 128:256]

    def piece(src, dst, s, r, unit, q, dev):
        rows = pl.ds(q * 128, 128)
        return rc(src.at[unit, rows], dst.at[unit, rows], s.at[unit, q], r.at[unit, q], dev)

    def to_mid(unit, q, dev):
        return piece(pe_send, pe_recv, e_s, e_r, unit, q, dev)

    def to_other(unit, q):
        return piece(pm_send, pm_recv, m_s, m_r, unit, q, other_mid)

    def to_end(unit, q, dev):
        return piece(scaled, scaled, c_s, c_r, unit, q, dev)

    def wait_scaled(unit, carry):
        for q in range(2):
            to_end(unit, q, mid_of_end).wait_recv()
        return carry

    def step(it, carry):
        @pl.when((it % 2 == 0) & (it < 2 * NB))
        def _():
            j = it // 2
            for d in (1, 2, 3):
                def put(k, v, d=d):
                    sbuf[j, d - 1, k * 256 : (k + 1) * 256, :] = v

                decode(j, (x + d) % 4, put)
                weights_x(j, d).start()

            def put_own(k, v):
                w[j, dp, 0, k * 256 : (k + 1) * 256, :] = v

            decode(j, x, put_own)
            forward(j, 0).start()

        @pl.when(it == 1)
        def _():
            for d in (1, 2, 3):
                token_x(1, d).start()
            for d in (1, 2, 3):
                token_x(0, d).wait_recv()
            for d in (1, 2, 3):
                token_y(0, d, y).start()

        @pl.when(it == 7)
        def _():
            for d in (1, 2, 3):
                src = (x + d) % 4
                rc(in_x.at[src], in_x.at[src], ix_s.at[d], ix_r.at[src], xpeer(d)).wait_recv()
            total = in_x[0].astype(f32) + in_x[1].astype(f32) + in_x[2].astype(f32) + in_x[3].astype(f32)
            in_z[z] = total.astype(bf16)
            for d in (1, 2, 3):
                rc(in_z.at[z], in_z.at[z], iz_s.at[d], iz_r.at[z], zpeer(d)).start()

        @pl.when(it == 11)
        def _():
            for d in (1, 2, 3):
                src = (z + d) % 4
                rc(in_z.at[src], in_z.at[src], iz_s.at[d], iz_r.at[src], zpeer(d)).wait_recv()
            total = in_z[0].astype(f32) + in_z[1].astype(f32) + in_z[2].astype(f32) + in_z[3].astype(f32)
            in_y[y] = total.astype(bf16)
            for d in (1, 2, 3):
                rc(in_y.at[y], in_y.at[y], iy_s.at[d], iy_r.at[y], ypeer(d)).start()

        @pl.when(it == PRE)
        def _():
            for d in (1, 2, 3):
                token_x(1, d).wait_recv()
            for d in (1, 2, 3):
                token_y(0, d, (y + d) % 4).wait_recv()
            for d in (1, 2, 3):
                token_y(1, d, y).start()

        @pl.when(it == PRE + 3)
        def _():
            for d in (1, 2, 3):
                token_y(1, d, (y + d) % 4).wait_recv()

        @pl.when((it >= PRE) & (it < PRE + 2 * NB))
        def _():
            j, h, unit = place(it - PRE)

            @pl.when(h == 0)
            def _():
                for rel in range(4):
                    rc(w.at[j, 1 - dp, rel], w.at[j, 1 - dp, rel], f_s.at[j, rel], f_r.at[j, rel], sibling).wait_recv()
                ss = None
                for s in range(4):
                    wide = jnp.concatenate([w[j, 0, s], w[j, 1, s]], axis=1).astype(f32)
                    sq = jnp.sum((wide * wide).reshape(64, 8, 256), axis=0)
                    ss = sq if ss is None else ss + sq
                ss_own[j] = ss

                @pl.when(is_end)
                def _():
                    rc(ss_own.at[j], ss_e.at[j], se_s.at[j], se_r.at[j], mid_of_end).start()

            part = None
            for s in range(4):
                both = jnp.concatenate([w[j, 0, s], w[j, 1, s]], axis=1)
                term = dot(tok[s, h].reshape(256, 512), both)
                part = term if part is None else part + term

            @pl.when(is_end)
            def _():
                pe_send[unit] = part.astype(bf16)
                for q in range(2):
                    to_mid(unit, q, mid_of_end).start()

            @pl.when(is_mid)
            def _():
                own_part[unit] = part

        early = (it >= PRE - 1) & (it < PRE + 2)
        late = (it % 2 == 0) & (it >= LEAD + 6) & (it < LEAD + 2 * NB)

        @pl.when(early | late)
        def _():
            j = jnp.where(early, it - (PRE - 1), (it - LEAD) // 2)
            for d in (1, 3, 2):
                weights_x(j, d).wait_recv()
                forward(j, 4 - d).start()

        @pl.when(is_mid & (it >= MIX) & (it < MIX + 2 * NB))
        def _():
            j, h, unit = place(it - MIX)

            @pl.when(h == 0)
            def _():
                rc(ss_own.at[j], ss_e.at[j], se_s.at[j], se_r.at[j], end_of_mid).wait_recv()
                ss_m_send[j] = ss_own[j] + ss_e[j]
                rc(ss_m_send.at[j], ss_m_recv.at[j], sm_s.at[j], sm_r.at[j], other_mid).start()

            for q in range(2):
                to_mid(unit, q, end_of_mid).wait_recv()
                rows = pl.ds(q * 128, 128)
                pm_send[unit, rows] = (own_part[unit, rows] + pe_recv[unit, rows].astype(f32)).astype(bf16)
                to_other(unit, q).start()

        @pl.when(it == GRAD)
        def _():
            grad_copy.wait()

        @pl.when(is_mid & (it >= GRAD) & (it < GRAD + 2 * NB))
        def _():
            j, h, unit = place(it - GRAD)

            @pl.when(h == 0)
            def _():
                rc(ss_m_send.at[j], ss_m_recv.at[j], sm_s.at[j], sm_r.at[j], other_mid).wait_recv()

            squares = jnp.sum(ss_m_send[j] + ss_m_recv[j], axis=0, keepdims=True)
            norm = jnp.sqrt(squares + norm_eps)
            cols = pl.ds(pl.multiple_of(x * (NB * LANES) + j * LANES, LANES), LANES)
            fac_g = mag_in_ref[0:1, cols] / norm[:, 0:128]
            fac_u = mag_in_ref[1:2, cols] / norm[:, 128:256]
            own_cols = pl.ds(pl.multiple_of(j * LANES, LANES), LANES)

            def chunk(n, sums):
                rows = pl.ds(pl.multiple_of(n * 64, 64), 64)
                token_rows = [pl.ds(pl.multiple_of(n * 128 + q * 64 + h * 32, 32), 32) for q in range(2)]
                pre = pm_send[unit, rows, :].astype(f32) + pm_recv[unit, rows, :].astype(f32)
                pre_g, pre_u = pre[:, 0:128], pre[:, 128:256]
                g, u = pre_g * fac_g, pre_u * fac_u
                s = 1.0 / (1.0 + jnp.exp(-g))
                go = jnp.concatenate([grads[q, own_cols] for q in token_rows], axis=0).astype(f32) * s
                dg = go * u * (1.0 + g * (1.0 - s))
                du = go * g
                scaled[unit, rows, 0:128] = (dg * fac_g).astype(bf16)
                scaled[unit, rows, 128:256] = (du * fac_u).astype(bf16)
                both = jnp.concatenate([dg * pre_g, du * pre_u], axis=1)
                return sums + jnp.sum(both.reshape(8, 8, 256), axis=0)

            sums = jnp.zeros((8, 256), f32)
            for q in range(2):
                to_other(unit, q).wait_recv()
                sums = lax.fori_loop(2 * q, 2 * q + 2, chunk, sums)
                to_end(unit, q, end_of_mid).start()
            mags[pl.ds(unit, 1), :] = jnp.sum(sums, axis=0, keepdims=True) / norm

        return carry

    lax.fori_loop(0, GRAD + 2 * NB, step, 0)

    @pl.when(is_mid)
    def _():
        rc(mags, mags_in, mg_s.at[0], mg_r.at[0], end_of_mid).start()

    @pl.when(is_end)
    def _():
        lax.fori_loop(0, 2 * NB - 3, wait_scaled, 0)
        wait_scaled(2 * NB - 2, 0)

    def x_sum(buf):
        return buf[0].astype(f32) + buf[1].astype(f32) + buf[2].astype(f32) + buf[3].astype(f32)

    def gather(buf, me, peer, send, recv):
        def start():
            for d in (1, 2, 3):
                rc(buf.at[me], buf.at[me], send.at[d], recv.at[me], peer(d)).start()

        def wait():
            for d in (1, 2, 3):
                src = (me + d) % 4
                rc(buf.at[src], buf.at[src], send.at[d], recv.at[src], peer(d)).wait_recv()

        return start, wait

    bx_start, bx_wait = gather(br_x, x, xpeer, bx_s, bx_r)
    by_start, by_wait = gather(br_y, y, ypeer, by_s, by_r)
    bz_start, bz_wait = gather(br_z, z, zpeer, bz_s, bz_r)
    ux_start, _ = gather(u_x, x, xpeer, ux_s, ux_r)

    def up_across(src):
        return rc(u_x.at[src], u_other.at[src], uo_s.at[src], uo_r.at[src], sibling)

    def ga(h, d):
        target = (x + d) % 4
        return rc(ga_send.at[h, target], ga_recv.at[h, x], ga_s.at[h, d], ga_r.at[h, x], xpeer(d))

    def gb(h, d):
        target = (y + d) % 4
        return rc(gb_send.at[h, target], gb_recv.at[h, y], gb_s.at[h, d], gb_r.at[h, y], ypeer(d))

    def ga2(h, d):
        target = (y + d) % 4
        return rc(ga2_send.at[h, target], ga2_recv.at[h, y], ga2_s.at[h, d], ga2_r.at[h, y], ypeer(d))

    def gb2(h, d):
        target = (x + d) % 4
        return rc(gb2_send.at[h, target], gb2_recv.at[h, x], gb2_s.at[h, d], gb2_r.at[h, x], xpeer(d))

    def gz(h):
        return rc(gz_send.at[h], gz_recv.at[h], gz_s.at[h], gz_r.at[h], zhpeer)

    def first(h, block_of):
        def back_block(n, carry):
            rel = (1 + n) % 4
            target = (x + rel) % 4
            out = block_of(rel).astype(bf16).reshape(4, 2, 32, 512)
            ga_send[h, target] = out[:, 0]
            gb_send[h, :, target] = out[:, 1]

            @pl.when(n < 3)
            def _():
                ga(h, rel).start()

            return carry

        lax.fori_loop(0, 4, back_block, 0)
        for d in (1, 2, 3):
            gb(h, d).start()

    def received(send, recv, h, me):
        acc = send[h, me].astype(f32)
        for d in (1, 2, 3):
            acc = acc + recv[h, (me + d) % 4].astype(f32)
        return acc

    def wait_from(h, me, s_sem, r_sem, send, recv, peer):
        for d in (1, 2, 3):
            src = (me + d) % 4
            rc(send.at[h, src], recv.at[h, src], s_sem.at[h, d], r_sem.at[h, src], peer(d)).wait_recv()

    def second(h):
        wait_from(h, x, ga_s, ga_r, ga_send, ga_recv, xpeer)
        ga2_send[h] = received(ga_send, ga_recv, h, x).astype(bf16)
        for d in (1, 2, 3):
            ga2(h, d).start()
        wait_from(h, y, gb_s, gb_r, gb_send, gb_recv, ypeer)
        gb2_send[h] = received(gb_send, gb_recv, h, y).astype(bf16)
        for d in (1, 2, 3):
            gb2(h, d).start()

    def third(h):
        wait_from(h, y, ga2_s, ga2_r, ga2_send, ga2_recv, ypeer)
        acc_a = received(ga2_send, ga2_recv, h, y)
        wait_from(h, x, gb2_s, gb2_r, gb2_send, gb2_recv, xpeer)
        acc_b = received(gb2_send, gb2_recv, h, x)
        gz_send[h] = jnp.where(zh == 0, acc_b, acc_a).astype(bf16)
        gz(h).start()
        gz_keep[h] = jnp.where(zh == 0, acc_a, acc_b)

    def last(h):
        gz(h).wait_recv()
        return (gz_keep[h] + gz_recv[h].astype(f32)).astype(bf16)

    first(0, lambda rel: token_terms(0, rel, range(NB)))

    for d in (1, 2, 3):
        src = (y + d) % 4
        rc(in_y.at[src], in_y.at[src], iy_s.at[d], iy_r.at[src], ypeer(d)).wait_recv()
    in_all = in_y[...].reshape(4, 2, 2, 32, LANES)
    for h in range(2):
        inner[h] = in_all[:, :, h].reshape(256, LANES)

    def early(n, carry):
        token_sum[n] = token_terms(1, n, range(NB - 2))
        return carry

    lax.fori_loop(0, 4, early, 0)
    rank_sum[0] = rank_terms(0, range(NB))
    rank_sum[1] = rank_terms(1, range(NB - 2))
    for j in range(NB - 2):
        up_term(j)

    @pl.when(is_end)
    def _():
        wait_scaled(2 * NB - 3, 0)
        wait_scaled(2 * NB - 1, 0)

    br_zh_send[0:64] = rank_sum[0].astype(bf16)
    br_zh_send[64:128] = (rank_sum[1] + rank_terms(1, range(NB - 2, NB))).astype(bf16)
    rc(br_zh_send, br_zh_recv, bh_s.at[0], bh_r.at[0], zhpeer).start()

    first(1, lambda rel: token_sum[rel] + token_terms(1, rel, range(NB - 2, NB)))

    for j in range(NB - 2, NB):
        up_term(j)

    @pl.when(is_end)
    def _():
        rc(mags, mags_in, mg_s.at[0], mg_r.at[0], mid_of_end).wait_recv()
        mags[...] = mags_in[...]

    for j in range(NB):
        for p in range(2):
            u_part[p, 64:72, j * LANES : (j + 1) * LANES] = jnp.broadcast_to(
                mags[2 * j : 2 * j + 1, p * 128 : (p + 1) * 128]
                + mags[2 * j + 1 : 2 * j + 2, p * 128 : (p + 1) * 128],
                (8, LANES),
            )
    rc(u_part.at[1 - dp], u_recv, ud_s.at[0], ud_r.at[0], sibling).start()

    for d in (1, 2, 3):
        for h in range(2):
            token_x(h, d).wait_send()
            token_y(h, d, y).wait_send()
        rc(in_x.at[x], in_x.at[x], ix_s.at[d], ix_r.at[x], xpeer(d)).wait_send()
        rc(in_z.at[z], in_z.at[z], iz_s.at[d], iz_r.at[z], zpeer(d)).wait_send()
        rc(in_y.at[y], in_y.at[y], iy_s.at[d], iy_r.at[y], ypeer(d)).wait_send()
    def drain(j, carry):
        for d in (1, 2, 3):
            weights_x(j, d).wait_send()
        for rel in range(4):
            forward(j, rel).wait_send()

        @pl.when(is_end)
        def _():
            rc(ss_own.at[j], ss_e.at[j], se_s.at[j], se_r.at[j], mid_of_end).wait_send()

        @pl.when(is_mid)
        def _():
            rc(ss_m_send.at[j], ss_m_recv.at[j], sm_s.at[j], sm_r.at[j], other_mid).wait_send()

        return carry

    def drain_unit(unit, carry):
        @pl.when(is_end)
        def _():
            for q in range(2):
                to_mid(unit, q, mid_of_end).wait_send()

        @pl.when(is_mid)
        def _():
            for q in range(2):
                to_other(unit, q).wait_send()
                to_end(unit, q, end_of_mid).wait_send()

        return carry

    lax.fori_loop(0, 2 * NB, drain_unit, 0)
    lax.fori_loop(0, NB, drain, 0)

    @pl.when(is_mid)
    def _():
        rc(mags, mags_in, mg_s.at[0], mg_r.at[0], end_of_mid).wait_send()

    second(0)
    rc(u_part.at[1 - dp], u_recv, ud_s.at[0], ud_r.at[0], sibling).wait_recv()
    u_x[x, 0:72] = (u_part[dp] + u_recv[...]).astype(bf16)
    u_x[x, 72:80] = jnp.zeros((8, NB * LANES), bf16)
    rc(br_zh_send, br_zh_recv, bh_s.at[0], bh_r.at[0], zhpeer).wait_recv()
    br_x[x] = (br_zh_send[...].astype(f32) + br_zh_recv[...].astype(f32)).astype(bf16)
    bx_start()
    third(0)
    bx_wait()
    br_y[y] = x_sum(br_x).astype(bf16)
    by_start()
    second(1)
    ux_start()
    up_across(x).start()
    by_wait()
    br_z[z] = x_sum(br_y).astype(bf16)
    bz_start()
    third(1)
    bz_wait()
    ranks = br_z[...].reshape(4, 2, 2, 32, LANES)
    for h in range(2):
        br_all[:, :, h] = ranks[:, h]
    dg_send[...] = adapter_scale * dot_tn(tokens_ref[...], br_all[...].reshape(512, LANES))
    rc(dg_send, dg_recv, dg_s.at[0], dg_r.at[0], sibling).start()

    for d in (1, 3, 2):
        src = (x + d) % 4
        rc(u_x.at[src], u_x.at[src], ux_s.at[d], ux_r.at[src], xpeer(d)).wait_recv()
        up_across(src).start()
    u_ref[dp] = u_x[...]
    for h in range(2):
        final = last(h)
        tg_ref[h * 32 : (h + 1) * 32, :] = dot(final, perm[...]).astype(bf16)
    rc(dg_send, dg_recv, dg_s.at[0], dg_r.at[0], sibling).wait_recv()
    dg_ref[...] = dg_send[...] + dg_recv[...]
    for src in range(4):
        up_across(src).wait_recv()
    u_ref[1 - dp] = u_other[...]

    for d in (1, 2, 3):
        rc(br_x.at[x], br_x.at[x], bx_s.at[d], bx_r.at[x], xpeer(d)).wait_send()
        rc(br_y.at[y], br_y.at[y], by_s.at[d], by_r.at[y], ypeer(d)).wait_send()
        rc(br_z.at[z], br_z.at[z], bz_s.at[d], bz_r.at[z], zpeer(d)).wait_send()
        rc(u_x.at[x], u_x.at[x], ux_s.at[d], ux_r.at[x], xpeer(d)).wait_send()
        for h in range(2):
            ga(h, d).wait_send()
            gb(h, d).wait_send()
            ga2(h, d).wait_send()
            gb2(h, d).wait_send()
    rc(br_zh_send, br_zh_recv, bh_s.at[0], bh_r.at[0], zhpeer).wait_send()
    for h in range(2):
        gz(h).wait_send()
    rc(u_part.at[1 - dp], u_recv, ud_s.at[0], ud_r.at[0], sibling).wait_send()
    for src in range(4):
        up_across(src).wait_send()
    rc(dg_send, dg_recv, dg_s.at[0], dg_r.at[0], sibling).wait_send()


def finish(tg_in, dg_in, u_in, tg_ref, dg_ref, ug_ref, mg_ref):
    tg_ref[...] = tg_in[...]
    dg_ref[...] = dg_in[...]
    for p in range(2):
        for s in range(4):
            lanes = slice(s * NB * LANES, (s + 1) * NB * LANES)
            ug_ref[p, :, lanes] = u_in[p, s, 0:64].astype(f32)
            mg_ref[p : p + 1, lanes] = u_in[p, s, 64:80].astype(f32)[0:1]


def shards(tokens, levels, scales, down, up, magnitude, grad):
    V = pltpu.VMEM
    D = pltpu.SemaphoreType.DMA
    NU = 2 * NB
    buffers = [
        V((256, 3584), jnp.int32), V((512, 896), bf16), V((4, 2, 4, 64, 512), bf16), V((512, 512), bf16),
        V((512, 128), bf16), V((512, 128), bf16), V((NB, 2, 4, 512, 128), bf16), V((NB, 3, 512, 128), bf16),
        V((NU, 256, 256), f32), V((NU, 256, 256), bf16), V((NU, 256, 256), bf16),
        V((NU, 256, 256), bf16), V((NU, 256, 256), bf16),
        V((NB, 8, 256), f32), V((NB, 8, 256), f32), V((NB, 8, 256), f32), V((NB, 8, 256), f32),
        V((NU, 256, 256), bf16), V((16, 256), f32), V((16, 256), f32),
        V((4, 128, 128), bf16), V((4, 128, 128), bf16), V((4, 128, 128), bf16), V((NB, 128, 256), bf16),
        V((2, 4, 4, 32, 512), bf16), V((2, 4, 4, 32, 512), bf16), V((2, 4, 4, 32, 512), bf16), V((2, 4, 4, 32, 512), bf16),
        V((2, 4, 32, 512), bf16), V((2, 4, 32, 512), bf16), V((2, 4, 32, 512), bf16), V((2, 4, 32, 512), bf16),
        V((2, 32, 512), f32), V((2, 32, 512), bf16), V((2, 32, 512), bf16),
        V((4, 128, 128), bf16), V((4, 128, 128), bf16), V((128, 128), bf16), V((128, 128), bf16),
        V((4, 128, 128), bf16), V((512, 128), f32), V((512, 128), f32),
        V((2, 72, 896), f32), V((72, 896), f32), V((4, 80, 896), bf16), V((4, 80, 896), bf16),
        V((2, 256, 128), bf16), V((4, 256, 512), f32), V((2, 64, 128), f32), V((4, 2, 2, 32, 128), bf16),
    ]
    sems = [D((2,)), D((2, 4)), D((2, 4)), D((2, 4)), D((2, 4)), D((NB, 4)), D((NB, 4))]
    sems += [D((NB, 4)), D((NB, 4)), D((NU, 2)), D((NU, 2)), D((NB,)), D((NB,))]
    sems += [D((NU, 2)), D((NU, 2)), D((NB,)), D((NB,)), D((NU, 2)), D((NU, 2)), D((1,)), D((1,))]
    sems += [D((4,))] * 6
    sems += [D((2, 4))] * 8 + [D((2,))] * 2
    sems += [D((4,)), D((4,)), D((4,)), D((4,)), D((1,)), D((1,)), D((4,)), D((4,)), D((1,)), D((1,))]
    sems += [D((1,)), D((1,)), D((4,)), D((4,)), D((4,)), D((4,))]
    vm = pl.BlockSpec(memory_space=pltpu.VMEM)
    hbm = pl.BlockSpec(memory_space=pl.ANY)
    token_out, down_out, up_out = pl.pallas_call(
        kernel,
        out_shape=(
            jax.ShapeDtypeStruct((64, 512), bf16),
            jax.ShapeDtypeStruct((512, 128), f32),
            jax.ShapeDtypeStruct((2, 4, 80, 896), bf16),
        ),
        in_specs=[vm, hbm, vm, vm, vm, vm, hbm],
        out_specs=(vm, vm, vm),
        scratch_shapes=buffers + sems,
        compiler_params=pltpu.CompilerParams(
            collective_id=0, has_side_effects=True, vmem_limit_bytes=56 * 1024 * 1024
        ),
        name="qdora_backward",
    )(tokens, levels, scales, down, up.reshape(128, 3584), magnitude, grad)
    return pl.pallas_call(
        finish,
        out_shape=(
            jax.ShapeDtypeStruct((64, 512), bf16),
            jax.ShapeDtypeStruct((512, 128), f32),
            jax.ShapeDtypeStruct((2, 64, 3584), f32),
            jax.ShapeDtypeStruct((2, 3584), f32),
        ),
        in_specs=[vm] * 3,
        out_specs=(vm,) * 4,
        name="write_outputs",
    )(token_out, down_out, up_out)


def solution(mesh):
    placed = (
        P("dp", "row"),
        P(None, "row", "col"),
        P(None, "row", "col"),
        P("row", None),
        P(None, None, "col"),
        P(None, "col"),
        P("dp", "col"),
    )
    return jax.shard_map(
        shards,
        mesh=mesh,
        in_specs=placed,
        out_specs=(P(("dp", "col"), "row"), P("row", None), P(None, None, "col"), P(None, "col")),
        check_vma=False,
    )
```
